512 devices in a mesh: expert: 8 (over y, core), etensor: 16 (over z), dp: 4 (over x).
Axes of the slice: x: 4, y: 4, z: 16, core: 2. Of those that a mesh axis runs over, the one named last changes fastest.
Arguments:
- tokens: bfloat16 [4096, 4096], P(('expert', 'dp'), 'etensor'), may hold values from -6 to 6
- out_grad: bfloat16 [4096, 4096], P(('expert', 'dp'), 'etensor'), may hold values from -6 to 6
- routes: int32 [4096, 2], P(('expert', 'dp')), may hold values from 0 to 7, all different within a row; in each aligned block of 128 rows (0 to 127, 128 to 255, ...) at most 36 rows name the same one
- gate_probs: float32 [4096, 2], P(('expert', 'dp')), may hold values from 0.1 to 1
- gate_weight: bfloat16 [8, 4096, 8192], P('expert', 'dp', 'etensor'), may hold values from -0.09375 to 0.09375
- up_weight: bfloat16 [8, 4096, 8192], P('expert', 'dp', 'etensor'), may hold values from -0.09375 to 0.09375
- down_weight: bfloat16 [8, 8192, 4096], P('expert', 'etensor', 'dp'), may hold values from -0.0625 to 0.0625
Outputs:
- input_grad: bfloat16 [4096, 4096], P(('expert', 'dp'), 'etensor')
- gate_grad: float32 [4096, 2], P(('expert', 'dp'))
The draws below stay inside these ranges and needn't reach their ends.
Inputs may be any that keep to these rules, and one draw needn't show every extreme that they name: `routes`: the two experts of a token differ. Within the 128 rows of one token group no expert is named by more than 36 rows, and in some group some expert is named by exactly 36 rows.
All inputs are finite; a program needn't handle non-finite values.
Results may differ from the reference program's by a relative error of at most 0.024.
Values may be sent and summed in bfloat16 or wider, within the bound.
No kernel may reach another device: no remote copies, remote signals or barrier semaphores. Data moves between devices by JAX's collectives and lax.ppermute only.
A program may use at most 64 MiB of HBM per device.

```python
import math
import jax
import jax.numpy as jnp
import numpy as np
from jax import lax

D = 4096
FF = 8192
TOK_DEV = 128
EXPERTS = 8
CAP = 36
TOKENS = 4096
N_EXPERT = 8
N_ETENSOR = 16
N_DP = 4


def block_scale(key, extent, split, low, largest):
    gain, own = 1.0, jax.random.fold_in(key, 6)
    for dim, parts in split:
        steps = jnp.exp(jax.random.uniform(jax.random.fold_in(own, dim), (parts,), jnp.float32, low / len(split), largest / len(split)))
        gain = gain * jnp.repeat(steps, extent[dim] // parts).reshape([-1 if axis == dim else 1 for axis in range(len(extent))])
    return gain


def deal_out(own_key, own, number, rows, number_of, top, limit, skew):
    sequence = jax.random.permutation(own_key, number_of)
    heavy_load, usual = load_shares(number_of, rows * top, limit, skew, True), load_shares(number_of, rows * top, limit, skew, False)
    places = jnp.arange(number_of)

    def named(sizes, rotation):
        used = int((sizes > 0).sum())
        fixed = max(1, used // 4)
        shifted = fixed + (places - fixed + rotation * (used - fixed)) % max(1, number_of - fixed)
        return jnp.zeros((number_of,), jnp.int32).at[sequence[jnp.where(places < fixed, places, shifted)]].set(jnp.asarray(sizes, jnp.int32))

    sizes = jnp.where(number % 4 == 0, named(heavy_load, number // 4), named(usual, number - number // 4 - 1))
    mixed = jax.random.permutation(jax.random.fold_in(own, 3), number_of)
    source_of, sink = mixed[0:number_of // 2 * 2:2], mixed[1:number_of // 2 * 2:2]
    margin = jnp.minimum(sizes[source_of] - 1, limit - sizes[sink]) // 2
    margin = jnp.where((source_of == sequence[0]) | (sink == sequence[0]) | (sizes[sink] == 0), 0, jnp.maximum(margin, 0))
    shifted = jax.random.randint(jax.random.fold_in(own, 4), (number_of // 2,), 0, 1 << 20) % (margin + 1)
    sizes = sizes.at[source_of].add(-shifted).at[sink].add(shifted)
    items = jnp.searchsorted(jnp.cumsum(sizes), jnp.arange(rows * top), side="right").astype(jnp.int32)
    grid = items.reshape(top, rows).T
    grid = grid[jax.random.permutation(jax.random.fold_in(own, 1), rows)]
    rotation = jax.random.randint(jax.random.fold_in(own, 2), (rows, 1), 0, top)
    return jnp.take_along_axis(grid, (jnp.arange(top)[None, :] + rotation) % top, axis=1)


def load_shares(amount, total, reach, lean, full):
    loads = [(1 << 20) // math.isqrt(standing ** lean) + 1 for standing in range(1, amount + 1)]
    largest = reach if full else min(reach, max(-(-total // amount), total * loads[0] // sum(loads)))
    least = 1 if total - largest >= amount - 1 else 0
    counts, surplus = [largest] + [least] * (amount - 1), total - largest - least * (amount - 1)
    while surplus > 0:
        movable = [i for i in range(1, amount) if counts[i] < largest] or [i for i in range(1, amount) if counts[i] < reach]
        whole, left = sum([loads[i] for i in movable]), surplus
        for i in movable:
            extra = min(reach - counts[i], max(1, left * loads[i] // whole), surplus)
            counts[i] = counts[i] + extra
            surplus = surplus - extra
    return np.array(counts)


def gaussian(stream_key, shape, deviation, bound, shards=(), kind=jnp.bfloat16):
    result = jax.random.normal(stream_key, shape, jnp.float32) * deviation
    if len(shards) > 0:
        result = block_scale(stream_key, shape, shards, -0.22, 0.18) * result
    return jnp.clip(result, min=-bound, max=bound).astype(kind)


def setup_inputs(seed: int = 0) -> dict:
    key_of = jax.random.split(jax.random.key(seed), 8)
    tokens = gaussian(key_of[0], (TOKENS, D), 1.0, 6.0, ((0, 32), (1, 16)))
    out_grad = gaussian(key_of[1], (TOKENS, D), 1.0, 6.0, ((0, 32), (1, 16)))
    routes_keys = jax.random.split(jax.random.fold_in(key_of[2], 1), TOKENS // TOK_DEV)
    routes_turns = jax.random.permutation(jax.random.fold_in(key_of[2], 3), TOKENS // TOK_DEV)
    routes = jax.vmap(lambda own, number: deal_out(jax.random.fold_in(key_of[2], 2), own, number, TOK_DEV, EXPERTS, 2, CAP, 2))(routes_keys, routes_turns).reshape((TOKENS, 2))
    gate_probs = jnp.clip(0.1 + 0.9 * jax.random.uniform(key_of[3], (TOKENS, 2), jnp.float32) ** block_scale(key_of[3], (TOKENS, 2), ((0, 32),), -0.2, 0.2), 0.1, 1.0)
    gate_weight = gaussian(key_of[4], (EXPERTS, D, FF), D ** -0.5, 0.09375, ((0, 8), (1, 4), (2, 16)))
    up_weight = gaussian(key_of[5], (EXPERTS, D, FF), D ** -0.5, 0.09375, ((0, 8), (1, 4), (2, 16)))
    down_weight = gaussian(key_of[6], (EXPERTS, FF, D), FF ** -0.5, 0.0625, ((0, 8), (1, 16), (2, 4)))
    return {"tokens": tokens, "out_grad": out_grad, "routes": routes, "gate_probs": gate_probs, "gate_weight": gate_weight, "up_weight": up_weight, "down_weight": down_weight}


def expert_backward(args):
    rows_x, rows_dy, w_gate, w_up, w_down = args
    width = rows_x.shape[-1]
    rows = rows_x.reshape(-1, width)
    grads = rows_dy.reshape(-1, width)
    gate_pre = jnp.dot(rows, w_gate, preferred_element_type=jnp.float32)
    up_pre = jnp.dot(rows, w_up, preferred_element_type=jnp.float32)
    back = jnp.dot(grads, w_down.T, preferred_element_type=jnp.float32)
    sig = jax.nn.sigmoid(gate_pre)
    act = gate_pre * sig
    hidden = act * up_pre
    gate_rows = jnp.sum(hidden * back, axis=1)
    d_gate = (back * up_pre * sig * (1.0 + gate_pre * (1.0 - sig))).astype(jnp.bfloat16)
    d_up = (back * act).astype(jnp.bfloat16)
    block = FF // N_ETENSOR

    def add_block(total, index):
        start = index * block
        term = jnp.dot(lax.dynamic_slice_in_dim(d_gate, start, block, 1),
                       lax.dynamic_slice_in_dim(w_gate, start, block, 1).T,
                       preferred_element_type=jnp.float32)
        term = term + jnp.dot(lax.dynamic_slice_in_dim(d_up, start, block, 1),
                              lax.dynamic_slice_in_dim(w_up, start, block, 1).T,
                              preferred_element_type=jnp.float32)
        rounded = lax.optimization_barrier(term.astype(jnp.bfloat16)).astype(jnp.float32)
        return total + rounded, None

    total, _ = lax.scan(add_block, jnp.zeros((rows.shape[0], width), jnp.float32),
                        jnp.arange(N_ETENSOR).astype(jnp.int32))
    groups = rows_x.shape[0]
    return total.astype(jnp.bfloat16).reshape(groups, CAP, width), gate_rows.reshape(groups, CAP)


def reference(tokens, out_grad, routes, gate_probs, gate_weight, up_weight, down_weight):
    groups = N_EXPERT * N_DP
    pairs = 2 * TOK_DEV
    flat = routes.reshape(groups, pairs).astype(jnp.int32)
    onehot = (flat[:, :, None] == jnp.arange(EXPERTS).astype(jnp.int32)[None, None, :]).astype(jnp.int32)
    ranks = jnp.cumsum(onehot, axis=1) - onehot
    slot = jnp.sum(ranks * onehot, axis=2).astype(jnp.int32)
    position = (flat * CAP + slot).astype(jnp.int32)
    group_ids = jnp.arange(groups).astype(jnp.int32)[:, None]
    table = jnp.full((groups, EXPERTS * CAP), pairs, jnp.int32)
    table = table.at[group_ids, position].set(jnp.broadcast_to(jnp.arange(pairs).astype(jnp.int32)[None, :], (groups, pairs)))

    def place(rows):
        doubled = jnp.repeat(rows.reshape(groups, TOK_DEV, D), 2, axis=1)
        padded = jnp.concatenate([doubled, jnp.zeros((groups, 1, D), rows.dtype)], axis=1)
        picked = jnp.take_along_axis(padded, table[:, :, None], axis=1)
        return jnp.transpose(picked.reshape(groups, EXPERTS, CAP, D), (1, 0, 2, 3))

    sent_x = place(tokens)
    sent_dy = place(out_grad)
    input_rows, gate_rows = lax.map(expert_backward, (sent_x, sent_dy, gate_weight, up_weight, down_weight))
    input_rows = jnp.transpose(input_rows, (1, 0, 2, 3)).reshape(groups, EXPERTS * CAP, D)
    gate_rows = jnp.transpose(gate_rows, (1, 0, 2)).reshape(groups, EXPERTS * CAP)
    row_grad = jnp.take_along_axis(input_rows, position[:, :, None], axis=1)
    gate_grad = jnp.take_along_axis(gate_rows, position, axis=1)
    probs = gate_probs.reshape(groups, pairs)
    weighted = row_grad.astype(jnp.float32) * probs[:, :, None]
    input_grad = jnp.sum(weighted.reshape(groups, TOK_DEV, 2, D), axis=2)
    return input_grad.reshape(TOKENS, D).astype(jnp.bfloat16), gate_grad.reshape(TOKENS, 2)
```

```python
import functools

import jax
import jax.numpy as jnp
from jax import lax
from jax.experimental import pallas as pl
from jax.experimental.pallas import tpu as pltpu
from jax.sharding import PartitionSpec as P

NT = (((1,), (1,)), ((), ()))


def expert_kernel(feat, ff, cap_rows, blocks, pitch, slots, slot_of, order, z_of, recv, *refs):
    weights, (out, rows_v, wg, wu, wd, sems) = refs[:15], refs[15:]
    per = blocks // 4
    half = wg.shape[1] // 2
    half_ff = wd.shape[1] // 2
    copies = []

    def start(src, dst):
        copy = pltpu.make_async_copy(src, dst, sems.at[len(copies)])
        copy.start()
        copies.append(copy)
        return copy

    waits = []
    for s in range(4):
        group = [start(recv.at[pl.ds(slot_of[s] * per, per)], rows_v.at[s])]
        if s < 3:
            g, u, d = weights[3 * s : 3 * s + 3]
            group += [start(g.at[0], wg.at[s]), start(u.at[0], wu.at[s]), start(d.at[0], wd.at[s])]
        else:
            g1, u1, d1, g2, u2, d2 = weights[9:]
            group += [
                start(g1, wg.at[s, pl.ds(0, half)]),
                start(u1, wu.at[s, pl.ds(0, half)]),
                start(d1, wd.at[s, pl.ds(0, half_ff)]),
                start(g2, wg.at[s, pl.ds(half, half)]),
                start(u2, wu.at[s, pl.ds(half, half)]),
                start(d2, wd.at[s, pl.ds(half_ff, half_ff)]),
            ]
        waits.append(group)

    gate_pre = up_pre = back = None
    for s in range(4):
        for copy in waits[s]:
            copy.wait()
        x = jnp.concatenate([rows_v[s, k, :, :feat] for k in range(per)], axis=1)
        y = jnp.concatenate([rows_v[s, k, :, feat:] for k in range(per)], axis=1)
        g = jnp.dot(x, wg[s], preferred_element_type=jnp.float32)
        u = jnp.dot(x, wu[s], preferred_element_type=jnp.float32)
        b = lax.dot_general(y, wd[s], NT, preferred_element_type=jnp.float32)
        gate_pre = g if s == 0 else gate_pre + g
        up_pre = u if s == 0 else up_pre + u
        back = b if s == 0 else back + b

    sig = 1.0 / (1.0 + jnp.exp(-gate_pre))
    act = gate_pre * sig
    prod = act * up_pre * back
    d_gate = (back * up_pre * sig * (1.0 + gate_pre * (1.0 - sig))).astype(jnp.bfloat16)
    d_up = (back * act).astype(jnp.bfloat16)

    ones = jnp.ones((16, prod.shape[1]), jnp.bfloat16)
    total = None
    rest = prod
    for _ in range(3):
        limb = rest.astype(jnp.bfloat16)
        rest = rest - limb.astype(jnp.float32)
        part = lax.dot_general(ones, limb, NT, preferred_element_type=jnp.float32)
        total = part if total is None else total + part
    top = total.astype(jnp.bfloat16).astype(jnp.float32)
    low = total - top
    over = cap_rows - feat
    row = lax.broadcasted_iota(jnp.int32, (16, feat), 0)
    lane = lax.broadcasted_iota(jnp.int32, (16, feat), 1)
    q = z_of[0]
    mine = (lane >= q * over) & (lane < (q + 1) * over)
    wide = lambda v: jnp.concatenate([v[:, feat:]] * (feat // over), axis=1)
    extra = jnp.where(row == q, top[:, :feat], 0.0)
    extra = jnp.where(row == q + slots, low[:, :feat], extra)
    extra = jnp.where((row == 2 * slots) & mine, wide(top), extra)
    extra = jnp.where((row == 2 * slots + 1) & mine, wide(low), extra)
    extra = extra.astype(jnp.bfloat16)
    for z in range(blocks):
        out[pl.ds(pitch * z + cap_rows, 16), :] = extra
        if pitch > cap_rows + 16 and pitch * (z + 1) <= out.shape[0]:
            out[pl.ds(pitch * z + cap_rows + 16, pitch - cap_rows - 16), :] = jnp.zeros(
                (pitch - cap_rows - 16, feat), jnp.bfloat16
            )
    for s in range(4):
        term = lax.dot_general(d_gate, wg[s], NT, preferred_element_type=jnp.float32)
        term = term + lax.dot_general(d_up, wu[s], NT, preferred_element_type=jnp.float32)
        for k in range(per):
            at = pl.multiple_of((slot_of[s] * per + k) * pitch, 16)
            out[pl.ds(at, cap_rows), :] = term[:, k * feat : (k + 1) * feat].astype(jnp.bfloat16)


def expert_part(recv, weights, x_index, z_index, pitch, out_rows, slots):
    blocks, cap_rows, both = recv.shape
    feat = both // 2
    ff = weights[0].shape[2]
    depth = weights[0].shape[1]
    slot_of = jnp.stack([x_index, (x_index + 3) % 4, (x_index + 1) % 4, (x_index + 2) % 4])
    order = slot_of
    z_of = jnp.reshape(z_index % slots, (1,)).astype(jnp.int32)
    smem = pl.BlockSpec(memory_space=pltpu.SMEM)
    return pl.pallas_call(
        functools.partial(expert_kernel, feat, ff, cap_rows, blocks, pitch, slots),
        out_shape=jax.ShapeDtypeStruct((out_rows, feat), jnp.bfloat16),
        in_specs=[smem, smem, smem] + [pl.BlockSpec(memory_space=pl.ANY)] * 16,
        out_specs=pl.BlockSpec(memory_space=pltpu.VMEM),
        scratch_shapes=[
            pltpu.VMEM((4, blocks // 4, cap_rows, both), jnp.bfloat16),
            pltpu.VMEM((4, depth, ff), jnp.bfloat16),
            pltpu.VMEM((4, depth, ff), jnp.bfloat16),
            pltpu.VMEM((4, ff, depth), jnp.bfloat16),
            pltpu.SemaphoreType.DMA((19,)),
        ],
        compiler_params=pltpu.CompilerParams(vmem_limit_bytes=48 * 1024 * 1024),
        cost_estimate=pl.CostEstimate(
            flops=10 * cap_rows * 4 * depth * ff, bytes_accessed=24 << 20, transcendentals=cap_rows * ff
        ),
    )(slot_of.astype(jnp.int32), order.astype(jnp.int32), z_of, recv, *weights)


def shift(value, axis, step):
    size = lax.axis_size(axis)
    return lax.ppermute(value, axis, [(i, (i + step) % size) for i in range(size)])


def shards(tokens, out_grad, routes, gate_probs, gate_weight, up_weight, down_weight):
    tok_rows, feat = tokens.shape
    owners = lax.axis_size("expert")
    blocks = lax.axis_size("etensor")
    experts = owners * gate_weight.shape[0]
    capacity = min(tok_rows, 9 * tok_rows // (4 * experts))
    x_index = lax.axis_index("dp")
    z_index = lax.axis_index("etensor")
    cap_rows = owners * capacity
    slots = 7

    own = (gate_weight, up_weight, down_weight)
    left = tuple(shift(w, "dp", 1) for w in own)
    right = tuple(shift(w, "dp", -1) for w in own)
    far_left = tuple(shift(w[0, : w.shape[1] // 2], "dp", 1) for w in left)
    far_right = tuple(shift(w[0, w.shape[1] // 2 :], "dp", -1) for w in right)

    expert_ids = jnp.arange(experts, dtype=jnp.int32)
    hot = ((routes[:, :1] == expert_ids) | (routes[:, 1:] == expert_ids)).astype(jnp.bfloat16)
    earlier = jnp.tril(jnp.ones((tok_rows, tok_rows), jnp.bfloat16), -1)
    ranks = jnp.dot(earlier, hot, preferred_element_type=jnp.float32).astype(jnp.int32)
    slot = jnp.stack(
        [jnp.sum(jnp.where(routes[:, k : k + 1] == expert_ids, ranks, 0), axis=1) for k in range(2)],
        axis=1,
    )
    position = routes * capacity + slot
    places = jnp.arange(cap_rows, dtype=jnp.int32)[:, None]
    dispatch = ((places == position[None, :, 0]) | (places == position[None, :, 1])).astype(
        jnp.bfloat16
    )
    both = jnp.concatenate([tokens, out_grad], axis=1)
    placed = jnp.dot(dispatch, both, preferred_element_type=jnp.float32).astype(jnp.bfloat16)
    part = lax.all_to_all(
        placed.reshape(experts, capacity, 2 * feat), "expert", split_axis=0, concat_axis=0, tiled=True
    )
    recv = lax.all_gather(part.reshape(cap_rows, 2 * feat), "etensor", axis=0, tiled=False)

    pitch = PITCH
    out_rows = blocks * pitch if ALIGNED else blocks * (pitch - 1)
    terms = expert_part(
        recv, own + left + right + far_left + far_right, x_index, z_index, pitch, out_rows, slots
    )
    summed = lax.psum_scatter(terms, "etensor", scatter_dimension=0, tiled=True)
    if not ALIGNED:
        summed = lax.dynamic_slice_in_dim(summed, z_index, cap_rows + 16, 0)
    extra = summed[cap_rows:].astype(jnp.float32)
    over = cap_rows - feat
    head = jnp.sum(extra[: 2 * slots], axis=0)
    tail = jnp.sum(extra[2 * slots :].reshape(2, feat // over, over)[:, :slots], axis=(0, 1))
    gate_rows = jnp.concatenate([head, tail])
    gate_top = gate_rows.astype(jnp.bfloat16)
    gate_low = (gate_rows - gate_top.astype(jnp.float32)).astype(jnp.bfloat16)
    gates = jnp.concatenate(
        [
            gate_top.reshape(owners, 1, capacity),
            gate_low.reshape(owners, 1, capacity),
            jnp.zeros((owners, 1, feat - 2 * capacity), jnp.bfloat16),
        ],
        axis=2,
    )
    payload = jnp.concatenate([summed[:cap_rows].reshape(owners, capacity, feat), gates], axis=1)
    came = lax.all_to_all(payload, "expert", split_axis=0, concat_axis=0, tiled=True)
    came_rows = came[:, :capacity].reshape(cap_rows, feat)
    came_gate = (
        came[:, capacity, :capacity].astype(jnp.float32)
        + came[:, capacity, capacity : 2 * capacity].astype(jnp.float32)
    ).reshape(cap_rows)
    flat = position.reshape(-1)
    picked = jnp.take(came_rows, flat, axis=0, mode="clip")
    picked_gate = jnp.take(came_gate, flat, axis=0, mode="clip")
    weighted = picked.astype(jnp.float32) * gate_probs.reshape(-1)[:, None]
    input_grad = jnp.sum(weighted.reshape(tok_rows, 2, feat), axis=1).astype(jnp.bfloat16)
    return (input_grad, picked_gate.reshape(tok_rows, 2))


PITCH = 320
ALIGNED = False


def solution(mesh):
    return jax.shard_map(
        shards,
        mesh=mesh,
        in_specs=(
            P(("expert", "dp"), "etensor"),
            P(("expert", "dp"), "etensor"),
            P(("expert", "dp"), None),
            P(("expert", "dp"), None),
            P("expert", "dp", "etensor"),
            P("expert", "dp", "etensor"),
            P("expert", "etensor", "dp"),
        ),
        out_specs=(P(("expert", "dp"), "etensor"), P(("expert", "dp"), None)),
        check_vma=False,
    )
```

```python
import functools

import jax
import jax.numpy as jnp
from jax import lax
from jax.experimental import pallas as pl
from jax.experimental.pallas import tpu as pltpu
from jax.sharding import PartitionSpec as P

NT = (((1,), (1,)), ((), ()))


HBM = pl.BlockSpec(memory_space=pltpu.HBM)
VMEM = pl.BlockSpec(memory_space=pltpu.VMEM)
SMEM = pl.BlockSpec(memory_space=pltpu.SMEM)


def fetch(src, dst, sem):
    copy = pltpu.make_async_copy(src, dst, sem)
    copy.start()
    copy.wait()


STEPS = (64, 32, 16, 8, 4, 2, 1)


def code_kernel(rows_hbm, coded, rows, sem):
    fetch(rows_hbm, rows, sem)
    owners, capacity, both = rows.shape
    feat = both // 2
    values = jnp.concatenate([rows[e].astype(jnp.float32) for e in range(owners)], axis=0)
    largest = jnp.max(jnp.abs(values), axis=0, keepdims=True)
    largest = jnp.concatenate(
        [
            jnp.broadcast_to(jnp.max(half, axis=1, keepdims=True), (1, feat))
            for half in (largest[:, :feat], largest[:, feat:])
        ],
        axis=1,
    )
    scale = jnp.ones((1, both), jnp.float32)
    power = jnp.zeros((1, both), jnp.int32)
    for step in STEPS:
        fits = largest * (2.0**step) <= 32000.0
        largest = jnp.where(fits, largest * (2.0**step), largest)
        scale = jnp.where(fits, scale * (2.0**step), scale)
        power = jnp.where(fits, power + step, power)
    whole = jnp.round(values * scale).astype(jnp.int32)
    tail = jnp.broadcast_to(power, (coded.shape[0] - owners * capacity, both))
    coded[...] = jnp.concatenate([whole, tail], axis=0).astype(jnp.int16)


def code(rows, lines):
    owners, capacity, both = rows.shape
    return pl.pallas_call(
        code_kernel,
        out_shape=jax.ShapeDtypeStruct((lines, both), jnp.int16),
        in_specs=[HBM],
        out_specs=VMEM,
        scratch_shapes=[pltpu.VMEM(rows.shape, rows.dtype), pltpu.SemaphoreType.DMA(())],
        compiler_params=pltpu.CompilerParams(vmem_limit_bytes=8 << 20),
    )(rows)


def decode(block, cap_rows):
    power = block[cap_rows:].astype(jnp.int32)[0:1]
    scale = jnp.ones(power.shape, jnp.float32)
    for step in STEPS:
        taken = power >= step
        scale = jnp.where(taken, scale * (0.5**step), scale)
        power = jnp.where(taken, power - step, power)
    return (block[:cap_rows].astype(jnp.int32).astype(jnp.float32) * scale).astype(jnp.bfloat16)


def back_kernel(cap_rows, coded, down, parts, coded_v, down_v, parts_v, sems):
    groups = parts.shape[0]
    per = coded.shape[0] // groups
    feat = coded.shape[2] // 2
    weight = pltpu.make_async_copy(down.at[0], down_v, sems.at[groups])
    weight.start()
    copies = [
        pltpu.make_async_copy(
            coded.at[pl.ds(per * g, per), :, pl.ds(feat, feat)], coded_v.at[g], sems.at[g]
        )
        for g in range(groups)
    ]
    for copy in copies:
        copy.start()
    weight.wait()
    sent = []
    for g in range(groups):
        copies[g].wait()
        y = jnp.concatenate([decode(coded_v[g, k], cap_rows) for k in range(per)], axis=1)
        parts_v[g] = lax.dot_general(y, down_v[...], NT, preferred_element_type=jnp.float32).astype(
            jnp.bfloat16
        )
        sent.append(pltpu.make_async_copy(parts_v.at[g], parts.at[g], sems.at[groups + 1 + g]))
        sent[g].start()
    for copy in sent:
        copy.wait()


def back_parts(coded, down, cap_rows, groups):
    blocks, lines, both = coded.shape
    _, ff, depth = down.shape
    return pl.pallas_call(
        functools.partial(back_kernel, cap_rows),
        out_shape=pltpu.HBM((groups, cap_rows, ff), jnp.bfloat16),
        in_specs=[HBM, HBM],
        out_specs=HBM,
        scratch_shapes=[
            pltpu.VMEM((groups, blocks // groups, lines, both // 2), jnp.int16),
            pltpu.VMEM((ff, depth), jnp.bfloat16),
            pltpu.VMEM((groups, cap_rows, ff), jnp.bfloat16),
            pltpu.SemaphoreType.DMA((2 * groups + 1,)),
        ],
        compiler_params=pltpu.CompilerParams(vmem_limit_bytes=24 << 20),
        cost_estimate=pl.CostEstimate(
            flops=2 * groups * cap_rows * depth * ff, bytes_accessed=5 << 20, transcendentals=0
        ),
    )(coded, down)


def hidden_kernel(cap_rows, slot_of, coded, *refs):
    weights, (gate_out, up_out, gate_pre, up_pre, rows_v, w_v, sems) = refs[:4], refs[4:]
    per = coded.shape[0] // 4
    feat = coded.shape[2] // 2
    waits = []
    for s in range(4):
        rows = coded.at[pl.ds(slot_of[s] * per, per), :, pl.ds(0, feat)]
        waits.append(
            [
                pltpu.make_async_copy(rows, rows_v.at[s], sems.at[2 * s]),
                pltpu.make_async_copy(weights[s], w_v.at[s], sems.at[2 * s + 1]),
            ]
        )
        for copy in waits[s]:
            copy.start()
    for s in range(4):
        for copy in waits[s]:
            copy.wait()
        x = jnp.concatenate([decode(rows_v[s, k], cap_rows) for k in range(per)], axis=1)
        g = jnp.dot(x, w_v[s, 0], preferred_element_type=jnp.float32)
        u = jnp.dot(x, w_v[s, 1], preferred_element_type=jnp.float32)
        if s == 0:
            gate_pre[...], up_pre[...] = g, u
        else:
            gate_pre[...] += g
            up_pre[...] += u
    sent = [
        pltpu.make_async_copy(gate_pre, gate_out, sems.at[8]),
        pltpu.make_async_copy(up_pre, up_out, sems.at[9]),
    ]
    for copy in sent:
        copy.start()
    for copy in sent:
        copy.wait()


def hidden_part(coded, weights, slot_of, cap_rows):
    blocks, lines, both = coded.shape
    _, depth, ff = weights[0].shape
    result = pltpu.HBM((cap_rows, ff), jnp.float32)
    return pl.pallas_call(
        functools.partial(hidden_kernel, cap_rows),
        out_shape=(result, result),
        in_specs=[SMEM] + [HBM] * 5,
        out_specs=(HBM, HBM),
        scratch_shapes=[
            pltpu.VMEM((cap_rows, ff), jnp.float32),
            pltpu.VMEM((cap_rows, ff), jnp.float32),
            pltpu.VMEM((4, blocks // 4, lines, both // 2), jnp.int16),
            pltpu.VMEM((4, 2, depth, ff), jnp.bfloat16),
            pltpu.SemaphoreType.DMA((10,)),
        ],
        compiler_params=pltpu.CompilerParams(vmem_limit_bytes=32 << 20),
        cost_estimate=pl.CostEstimate(
            flops=4 * cap_rows * 4 * depth * ff, bytes_accessed=12 << 20, transcendentals=0
        ),
    )(slot_of, coded, *weights)


def term_kernel(pitch, slots, slot_of, z_of, gate_hbm, up_hbm, backs_hbm, *refs):
    weights, (out, gate_ref, up_ref, backs, w_v, out_v, blank, sems) = refs[:4], refs[4:]
    cap_rows = gate_ref.shape[0]
    feat = out.shape[1]
    per = w_v.shape[2] // feat
    first = [
        pltpu.make_async_copy(src, dst, sems.at[4 + i])
        for i, (src, dst) in enumerate(((gate_hbm, gate_ref), (up_hbm, up_ref), (backs_hbm, backs)))
    ]
    for copy in first:
        copy.start()
    waits = [pltpu.make_async_copy(weights[s], w_v.at[s], sems.at[s]) for s in range(4)]
    for copy in waits:
        copy.start()
    for copy in first:
        copy.wait()
    gate_pre, up_pre = gate_ref[...], up_ref[...]
    for s in range(4):
        b = backs[s].astype(jnp.float32)
        back = b if s == 0 else back + b
    sig = 1.0 / (1.0 + jnp.exp(-gate_pre))
    act = gate_pre * sig
    prod = act * up_pre * back
    d_gate = (back * up_pre * sig * (1.0 + gate_pre * (1.0 - sig))).astype(jnp.bfloat16)
    d_up = (back * act).astype(jnp.bfloat16)

    ones = jnp.ones((16, prod.shape[1]), jnp.bfloat16)
    total = None
    rest = prod
    for _ in range(3):
        limb = rest.astype(jnp.bfloat16)
        rest = rest - limb.astype(jnp.float32)
        part = lax.dot_general(ones, limb, NT, preferred_element_type=jnp.float32)
        total = part if total is None else total + part
    top = total.astype(jnp.bfloat16).astype(jnp.float32)
    low = total - top
    over = cap_rows - feat
    row = lax.broadcasted_iota(jnp.int32, (16, feat), 0)
    lane = lax.broadcasted_iota(jnp.int32, (16, feat), 1)
    q = z_of[0]
    mine = (lane >= q * over) & (lane < (q + 1) * over)
    wide = lambda v: jnp.concatenate([v[:, feat:]] * (feat // over), axis=1)
    extra = jnp.where(row == q, top[:, :feat], 0.0)
    extra = jnp.where(row == q + slots, low[:, :feat], extra)
    extra = jnp.where((row == 2 * slots) & mine, wide(top), extra)
    extra = jnp.where((row == 2 * slots + 1) & mine, wide(low), extra)
    extra = extra.astype(jnp.bfloat16)
    tail = pitch - cap_rows - 16
    span = per * pitch - tail
    blank[...] = jnp.zeros(blank.shape, blank.dtype)
    sent = []
    for j in range(3):
        sent.append(
            pltpu.make_async_copy(
                blank, out.at[pl.ds(j * per * pitch + span, tail)], sems.at[11 + j]
            )
        )
        sent[j].start()
    for s in range(4):
        waits[s].wait()
        term = lax.dot_general(d_gate, w_v[s, 0], NT, preferred_element_type=jnp.float32)
        term = term + lax.dot_general(d_up, w_v[s, 1], NT, preferred_element_type=jnp.float32)
        for k in range(per):
            at = k * pitch
            out_v[s, at : at + cap_rows] = term[:, k * feat : (k + 1) * feat].astype(jnp.bfloat16)
            out_v[s, at + cap_rows : at + cap_rows + 16] = extra
            if k + 1 < per:
                out_v[s, at + cap_rows + 16 : at + pitch] = jnp.zeros((tail, feat), jnp.bfloat16)
        at = pl.multiple_of(slot_of[s] * (per * pitch), 16)
        sent.append(pltpu.make_async_copy(out_v.at[s], out.at[pl.ds(at, span)], sems.at[7 + s]))
        sent[3 + s].start()
    for copy in sent:
        copy.wait()


def term_part(gate_pre, up_pre, backs, weights, slot_of, z_index, feat, pitch, out_rows, slots):
    cap_rows, ff = gate_pre.shape
    depth = weights[0].shape[1]
    z_of = jnp.reshape(z_index % slots, (1,)).astype(jnp.int32)
    per = depth // feat
    return pl.pallas_call(
        functools.partial(term_kernel, pitch, slots),
        out_shape=pltpu.HBM((out_rows, feat), jnp.bfloat16),
        in_specs=[SMEM, SMEM] + [HBM] * 7,
        out_specs=HBM,
        scratch_shapes=[
            pltpu.VMEM((cap_rows, ff), jnp.float32),
            pltpu.VMEM((cap_rows, ff), jnp.float32),
            pltpu.VMEM((4, cap_rows, ff), jnp.bfloat16),
            pltpu.VMEM((4, 2, depth, ff), jnp.bfloat16),
            pltpu.VMEM((4, per * pitch - 16, feat), jnp.bfloat16),
            pltpu.VMEM((16, feat), jnp.bfloat16),
            pltpu.SemaphoreType.DMA((14,)),
        ],
        compiler_params=pltpu.CompilerParams(vmem_limit_bytes=40 << 20),
        cost_estimate=pl.CostEstimate(
            flops=4 * cap_rows * 4 * depth * ff, bytes_accessed=14 << 20, transcendentals=cap_rows * ff
        ),
    )(slot_of, z_of, gate_pre, up_pre, backs, *weights)


def place_kernel(capacity, routes, tokens, moved_hbm, placed, slot, moved, sem):
    fetch(moved_hbm, moved, sem)
    tok_rows, feat = tokens.shape
    experts = placed.shape[0]
    ids = lax.broadcasted_iota(jnp.int32, (16, tok_rows), 0)
    place_of = lax.broadcasted_iota(jnp.int32, (48, tok_rows), 0)
    before = lax.broadcasted_iota(jnp.int32, (tok_rows, tok_rows), 0) < lax.broadcasted_iota(
        jnp.int32, (tok_rows, tok_rows), 1
    )
    as_ones = lambda mask: jnp.where(mask, 1.0, 0.0).astype(jnp.bfloat16)

    def slots_of(first, second):
        hot = (first == ids) | (second == ids)
        ranks = jnp.dot(as_ones(hot), as_ones(before), preferred_element_type=jnp.float32)
        return [
            jnp.sum(jnp.where(r == ids, ranks, 0.0), axis=0, keepdims=True).astype(jnp.int32)
            for r in (first, second)
        ]

    far = moved[tok_rows:].astype(jnp.float32).astype(jnp.int32)
    kinds = []
    for first, second, rows in (
        (routes[0:1, :], routes[1:2, :], tokens[...]),
        (far[0:1, :tok_rows], far[1:2, :tok_rows], moved[:tok_rows]),
    ):
        kinds.append((first, second, slots_of(first, second), rows))
    slot[...] = jnp.concatenate(kinds[0][2], axis=0)
    for e in range(experts):
        found = []
        for first, second, slots, rows in kinds:
            wanted = jnp.where(first == e, slots[0], jnp.where(second == e, slots[1], -1))
            found.append(
                jnp.dot(as_ones(wanted == place_of), rows, preferred_element_type=jnp.float32)
            )
        placed[e] = jnp.concatenate(found, axis=1)[:capacity].astype(jnp.bfloat16)


def place(routes, tokens, moved, experts, capacity):
    tok_rows, feat = tokens.shape
    vmem = pl.BlockSpec(memory_space=pltpu.VMEM)
    return pl.pallas_call(
        functools.partial(place_kernel, capacity),
        out_shape=(
            jax.ShapeDtypeStruct((experts, capacity, 2 * feat), jnp.bfloat16),
            jax.ShapeDtypeStruct((2, tok_rows), jnp.int32),
        ),
        in_specs=[vmem, vmem, HBM],
        out_specs=(vmem, vmem),
        scratch_shapes=[pltpu.VMEM(moved.shape, moved.dtype), pltpu.SemaphoreType.DMA(())],
        compiler_params=pltpu.CompilerParams(vmem_limit_bytes=8 << 20),
    )(routes, tokens, moved)


def pack_kernel(owners, capacity, slots, z_of, summed, payload, wide):
    feat = summed.shape[1]
    cap_rows = owners * capacity
    over = cap_rows - feat
    count = wide.shape[0]
    wide[pl.ds(0, summed.shape[0]), :] = summed[...].astype(jnp.float32)
    lined = pltpu.roll(wide[...], lax.rem(count - z_of[0], count), 0)
    extra = lined[cap_rows : cap_rows + 16]
    row = lax.broadcasted_iota(jnp.int32, (16, feat), 0)
    lane = lax.broadcasted_iota(jnp.int32, (16, feat), 1)
    head = jnp.sum(jnp.where(row < 2 * slots, extra, 0.0), axis=0, keepdims=True)
    tail = jnp.sum(
        jnp.where((row >= 2 * slots) & (lane < slots * over), extra, 0.0), axis=0, keepdims=True
    )
    tail = sum(tail[:, over * q : over * (q + 1)] for q in range(slots))
    gates = jnp.concatenate([head, tail], axis=1)
    top = gates.astype(jnp.bfloat16).astype(jnp.float32)
    low = gates - top
    blank = jnp.zeros((1, feat - 2 * capacity), jnp.float32)
    rest = jnp.zeros((payload.shape[1] - capacity - 1, feat), jnp.float32)
    for d in range(owners):
        cut = slice(capacity * d, capacity * (d + 1))
        line = jnp.concatenate([top[:, cut], low[:, cut], blank], axis=1)
        rows = lined[capacity * d : capacity * (d + 1)]
        payload[d] = jnp.concatenate([rows, line, rest], axis=0).astype(jnp.bfloat16)


def pack(summed, z_index, owners, capacity, slots, lines):
    rows, feat = summed.shape
    vmem = pl.BlockSpec(memory_space=pltpu.VMEM)
    return pl.pallas_call(
        functools.partial(pack_kernel, owners, capacity, slots),
        out_shape=jax.ShapeDtypeStruct((owners, lines, feat), jnp.bfloat16),
        in_specs=[pl.BlockSpec(memory_space=pltpu.SMEM), vmem],
        out_specs=vmem,
        scratch_shapes=[pltpu.VMEM((rows + 1, feat), jnp.float32)],
    )(jnp.reshape(z_index, (1,)).astype(jnp.int32), summed)


def combine_kernel(capacity, routes, slot, probs, came_hbm, input_grad, gate_grad, came, sem):
    fetch(came_hbm, came, sem)
    tok_rows = routes.shape[1]
    experts, lines, feat = came.shape
    flat = came[...].reshape(experts * lines, feat)
    place_of = lax.broadcasted_iota(jnp.int32, (experts * lines, tok_rows), 0)
    weight = jnp.zeros(place_of.shape, jnp.float32)
    for k in range(2):
        at = routes[k : k + 1, :] * lines + slot[k : k + 1, :]
        weight = jnp.where(place_of == at, probs[k : k + 1, :], weight)
    total = None
    for _ in range(3):
        limb = weight.astype(jnp.bfloat16)
        weight = weight - limb.astype(jnp.float32)
        part = lax.dot_general(
            limb, flat, (((0,), (0,)), ((), ())), preferred_element_type=jnp.float32
        )
        total = part if total is None else total + part
    input_grad[...] = total.astype(jnp.bfloat16)

    gates = jnp.concatenate(
        [came[e, 32:48].astype(jnp.float32)[capacity - 32 : capacity - 31] for e in range(experts)], axis=0
    ).astype(jnp.bfloat16)
    lane_of = lax.broadcasted_iota(jnp.int32, (feat, tok_rows), 0)
    ids = lax.broadcasted_iota(jnp.int32, (experts, tok_rows), 0)
    lines_of = []
    for k in range(2):
        s = slot[k : k + 1, :]
        pick = jnp.where((lane_of == s) | (lane_of == s + capacity), 1.0, 0.0).astype(jnp.bfloat16)
        values = jnp.dot(gates, pick, preferred_element_type=jnp.float32)
        lines_of.append(
            jnp.sum(jnp.where(routes[k : k + 1, :] == ids, values, 0.0), axis=0, keepdims=True)
        )
    gate_grad[...] = jnp.concatenate(lines_of, axis=0)


def combine(routes, slot, probs, came, capacity):
    tok_rows = routes.shape[1]
    feat = came.shape[2]
    vmem = pl.BlockSpec(memory_space=pltpu.VMEM)
    return pl.pallas_call(
        functools.partial(combine_kernel, capacity),
        out_shape=(
            jax.ShapeDtypeStruct((tok_rows, feat), jnp.bfloat16),
            jax.ShapeDtypeStruct((2, tok_rows), jnp.float32),
        ),
        in_specs=[vmem] * 3 + [HBM],
        out_specs=(vmem, vmem),
        scratch_shapes=[pltpu.VMEM(came.shape, came.dtype), pltpu.SemaphoreType.DMA(())],
        compiler_params=pltpu.CompilerParams(vmem_limit_bytes=8 << 20),
    )(routes, slot, probs, came)


def shift(value, axis, step):
    size = lax.axis_size(axis)
    return lax.ppermute(value, axis, [(i, (i + step) % size) for i in range(size)])


def shards(tokens, out_grad, routes, gate_probs, gate_weight, up_weight, down_weight):
    tok_rows, feat = tokens.shape
    owners = lax.axis_size("expert")
    blocks = lax.axis_size("etensor")
    experts = owners * gate_weight.shape[0]
    capacity = min(tok_rows, 9 * tok_rows // (4 * experts))
    x_index = lax.axis_index("dp")
    z_index = lax.axis_index("etensor")
    cap_rows = owners * capacity
    slots = 7

    columns = lax.axis_size("dp")
    gate_up = jnp.concatenate([gate_weight, up_weight], axis=0)

    per = blocks // columns
    swap = [
        ((columns * a + w) * columns + x, (columns * x + w) * columns + a)
        for a in range(columns)
        for w in range(per)
        for x in range(columns)
    ]
    tags = jnp.pad(routes.T.astype(jnp.bfloat16), ((0, 14), (0, feat - tok_rows)))
    moved = lax.ppermute(jnp.concatenate([out_grad, tags], axis=0), ("etensor", "dp"), swap)

    def send():
        placed, slot = place(routes.T, tokens, moved, experts, capacity)
        part = lax.all_to_all(placed, "expert", split_axis=0, concat_axis=0, tiled=True)
        return code(part, cap_rows + 16), slot

    coded, slot = lax.cond(
        routes[0, 0] >= 0,
        send,
        lambda: (
            jnp.zeros((cap_rows + 16, 2 * feat), jnp.int16),
            jnp.zeros((2, tok_rows), jnp.int32),
        ),
    )
    coded = lax.all_gather(coded, "etensor", axis=0, tiled=False)
    coded = pltpu.with_memory_space_constraint(coded, pltpu.HBM)
    backs = lax.all_to_all(
        back_parts(coded, down_weight, cap_rows, columns), "dp", split_axis=0, concat_axis=0, tiled=True
    )

    weights = (gate_up,) + tuple(shift(gate_up, "dp", step) for step in (1, -1, 2))
    slot_of = jnp.stack([(x_index + step) % 4 for step in (0, 3, 1, 2)]).astype(jnp.int32)
    gate_pre, up_pre = (
        pltpu.with_memory_space_constraint(v, pltpu.HBM)
        for v in hidden_part(coded, weights, slot_of, cap_rows)
    )
    pitch = cap_rows + 32
    terms = term_part(
        gate_pre, up_pre, backs, weights, slot_of, z_index, feat, pitch, blocks * (pitch - 1), slots
    )
    summed = lax.psum_scatter(terms, "etensor", scatter_dimension=0, tiled=True)
    payload = pack(summed, z_index, owners, capacity, slots, 48)
    came = lax.all_to_all(payload, "expert", split_axis=0, concat_axis=0, tiled=True)
    input_grad, gate_grad = combine(routes.T, slot, gate_probs.T, came, capacity)
    return input_grad, gate_grad.T


def solution(mesh):
    return jax.shard_map(
        shards,
        mesh=mesh,
        in_specs=(
            P(("expert", "dp"), "etensor"),
            P(("expert", "dp"), "etensor"),
            P(("expert", "dp"), None),
            P(("expert", "dp"), None),
            P("expert", "dp", "etensor"),
            P("expert", "dp", "etensor"),
            P("expert", "etensor", "dp"),
        ),
        out_specs=(P(("expert", "dp"), "etensor"), P(("expert", "dp"), None)),
        check_vma=False,
    )
```

```python
import functools

import jax
import jax.numpy as jnp
from jax import lax
from jax.experimental import pallas as pl
from jax.experimental.pallas import tpu as pltpu
from jax.sharding import PartitionSpec as P

NT = (((1,), (1,)), ((), ()))


HBM = pl.BlockSpec(memory_space=pltpu.HBM)
VMEM = pl.BlockSpec(memory_space=pltpu.VMEM)
SMEM = pl.BlockSpec(memory_space=pltpu.SMEM)


def fetch(src, dst, sem):
    copy = pltpu.make_async_copy(src, dst, sem)
    copy.start()
    copy.wait()


STEPS = (64, 32, 16, 8, 4, 2, 1)


def code_kernel(rows_hbm, coded, rows, sem):
    fetch(rows_hbm, rows, sem)
    owners, capacity, both = rows.shape
    feat = both // 2
    values = jnp.concatenate([rows[e].astype(jnp.float32) for e in range(owners)], axis=0)
    count = owners * capacity
    tails = []
    for i, half in enumerate((values[:, feat:], values[:, :feat])):
        largest = jnp.max(jnp.max(jnp.abs(half), axis=0, keepdims=True), axis=1, keepdims=True)
        largest = jnp.broadcast_to(largest, (1, feat))
        scale = jnp.ones((1, feat), jnp.float32)
        power = jnp.zeros((1, feat), jnp.int32)
        for step in STEPS:
            fits = largest * (2.0**step) <= 32000.0
            largest = jnp.where(fits, largest * (2.0**step), largest)
            scale = jnp.where(fits, scale * (2.0**step), scale)
            power = jnp.where(fits, power + step, power)
        whole = jnp.round(half * scale).astype(jnp.int32)
        coded[i * count : (i + 1) * count] = whole.astype(jnp.int16)
        tails.append(jnp.broadcast_to(power, (8, feat)))
    coded[2 * count :] = jnp.concatenate(tails, axis=0).astype(jnp.int16)


def code(rows):
    owners, capacity, both = rows.shape
    feat = both // 2
    return pl.pallas_call(
        code_kernel,
        out_shape=jax.ShapeDtypeStruct((2 * owners * capacity + 16, feat), jnp.int16),
        in_specs=[HBM],
        out_specs=VMEM,
        scratch_shapes=[pltpu.VMEM(rows.shape, rows.dtype), pltpu.SemaphoreType.DMA(())],
        compiler_params=pltpu.CompilerParams(vmem_limit_bytes=8 << 20),
    )(rows)


def decode(block, tail, row):
    power = tail.astype(jnp.int32)[row : row + 1]
    scale = jnp.ones(power.shape, jnp.float32)
    for step in STEPS:
        taken = power >= step
        scale = jnp.where(taken, scale * (0.5**step), scale)
        power = jnp.where(taken, power - step, power)
    return (block.astype(jnp.int32).astype(jnp.float32) * scale).astype(jnp.bfloat16)


def back_kernel(coded, down, parts, coded_v, tails_v, down_v, parts_v, sems):
    groups = parts.shape[0]
    per = coded.shape[0] // groups
    cap_rows = parts.shape[1]
    weight = pltpu.make_async_copy(down.at[0], down_v, sems.at[groups])
    tails = pltpu.make_async_copy(
        coded.at[:, pl.ds(2 * cap_rows, 16)], tails_v, sems.at[2 * groups + 1]
    )
    tails.start()
    weight.start()
    copies = [
        pltpu.make_async_copy(
            coded.at[pl.ds(per * g, per), pl.ds(0, cap_rows)], coded_v.at[g], sems.at[g]
        )
        for g in range(groups)
    ]
    for copy in copies:
        copy.start()
    tails.wait()
    weight.wait()
    sent = []
    for g in range(groups):
        copies[g].wait()
        y = jnp.concatenate([decode(coded_v[g, k], tails_v[per * g + k], 0) for k in range(per)], axis=1)
        parts_v[g] = lax.dot_general(y, down_v[...], NT, preferred_element_type=jnp.float32).astype(
            jnp.bfloat16
        )
        sent.append(pltpu.make_async_copy(parts_v.at[g], parts.at[g], sems.at[groups + 1 + g]))
        sent[g].start()
    for copy in sent:
        copy.wait()


def back_parts(coded, down, cap_rows, groups):
    blocks, lines, feat = coded.shape
    _, ff, depth = down.shape
    return pl.pallas_call(
        back_kernel,
        out_shape=pltpu.HBM((groups, cap_rows, ff), jnp.bfloat16),
        in_specs=[HBM, HBM],
        out_specs=HBM,
        scratch_shapes=[
            pltpu.VMEM((groups, blocks // groups, cap_rows, feat), jnp.int16),
            pltpu.VMEM((blocks, 16, feat), jnp.int16),
            pltpu.VMEM((ff, depth), jnp.bfloat16),
            pltpu.VMEM((groups, cap_rows, ff), jnp.bfloat16),
            pltpu.SemaphoreType.DMA((2 * groups + 2,)),
        ],
        compiler_params=pltpu.CompilerParams(vmem_limit_bytes=24 << 20),
        cost_estimate=pl.CostEstimate(
            flops=2 * groups * cap_rows * depth * ff, bytes_accessed=5 << 20, transcendentals=0
        ),
    )(coded, down)


def hidden_kernel(cap_rows, slot_of, coded, *refs):
    weights, (mixed, mixed_v, rows_v, tails_v, w_v, sems) = refs[:4], refs[4:]
    per = coded.shape[0] // 4
    ff = mixed.shape[2]
    waits = []
    for s in range(4):
        blocks = coded.at[pl.ds(slot_of[s] * per, per)]
        rows, tails = blocks.at[:, pl.ds(cap_rows, cap_rows)], blocks.at[:, pl.ds(2 * cap_rows, 16)]
        waits.append(
            [
                pltpu.make_async_copy(tails, tails_v.at[s], sems.at[9 + s]),
                pltpu.make_async_copy(rows, rows_v.at[s], sems.at[2 * s]),
                pltpu.make_async_copy(weights[s], w_v.at[s], sems.at[2 * s + 1]),
            ]
        )
        for copy in waits[s]:
            copy.start()
    total = None
    for s in range(4):
        for copy in waits[s]:
            copy.wait()
        x = jnp.concatenate([decode(rows_v[s, k], tails_v[s, k], 8) for k in range(per)], axis=1)
        part = jnp.dot(x, w_v[s], preferred_element_type=jnp.float32)
        total = part if s == 0 else total + part
    gate_pre, up_pre = total[:, :ff], total[:, ff:]
    sig = 1.0 / (1.0 + jnp.exp(-gate_pre))
    act = gate_pre * sig
    mixed_v[0] = up_pre * sig * (1.0 + gate_pre * (1.0 - sig))
    mixed_v[1] = act
    mixed_v[2] = act * up_pre
    sent = pltpu.make_async_copy(mixed_v, mixed, sems.at[8])
    sent.start()
    sent.wait()


def hidden_part(coded, weights, slot_of, cap_rows):
    blocks, lines, feat = coded.shape
    depth, wide = weights[0].shape
    return pl.pallas_call(
        functools.partial(hidden_kernel, cap_rows),
        out_shape=pltpu.HBM((3, cap_rows, wide // 2), jnp.float32),
        in_specs=[SMEM] + [HBM] * 5,
        out_specs=HBM,
        scratch_shapes=[
            pltpu.VMEM((3, cap_rows, wide // 2), jnp.float32),
            pltpu.VMEM((4, blocks // 4, cap_rows, feat), jnp.int16),
            pltpu.VMEM((4, blocks // 4, 16, feat), jnp.int16),
            pltpu.VMEM((4, depth, wide), jnp.bfloat16),
            pltpu.SemaphoreType.DMA((13,)),
        ],
        compiler_params=pltpu.CompilerParams(vmem_limit_bytes=32 << 20),
        cost_estimate=pl.CostEstimate(
            flops=8 * cap_rows * depth * wide,
            bytes_accessed=12 << 20,
            transcendentals=cap_rows * wide // 2,
        ),
    )(slot_of, coded, *weights)


def term_kernel(pitch, slots, slot_of, z_of, mixed_hbm, backs_hbm, *refs):
    weights, (out, mixed, backs, w_v, out_v, blank, sems) = refs[:4], refs[4:]
    cap_rows = mixed.shape[1]
    feat = out.shape[1]
    per = w_v.shape[1] // feat
    first = [
        pltpu.make_async_copy(backs_hbm, backs, sems.at[4]),
        pltpu.make_async_copy(mixed_hbm, mixed, sems.at[5]),
    ]
    for copy in first:
        copy.start()
    waits = [pltpu.make_async_copy(weights[s], w_v.at[s], sems.at[s]) for s in range(4)]
    for copy in waits:
        copy.start()
    for copy in first:
        copy.wait()
    for s in range(4):
        b = backs[s].astype(jnp.float32)
        back = b if s == 0 else back + b
    prod = mixed[2] * back
    sides = jnp.concatenate(
        [(back * mixed[0]).astype(jnp.bfloat16), (back * mixed[1]).astype(jnp.bfloat16)], axis=1
    )

    ones = jnp.ones((16, prod.shape[1]), jnp.bfloat16)
    total = None
    rest = prod
    for _ in range(3):
        limb = rest.astype(jnp.bfloat16)
        rest = rest - limb.astype(jnp.float32)
        part = lax.dot_general(ones, limb, NT, preferred_element_type=jnp.float32)
        total = part if total is None else total + part
    top = total.astype(jnp.bfloat16).astype(jnp.float32)
    low = total - top
    over = cap_rows - feat
    row = lax.broadcasted_iota(jnp.int32, (16, feat), 0)
    lane = lax.broadcasted_iota(jnp.int32, (16, feat), 1)
    q = z_of[0]
    mine = (lane >= q * over) & (lane < (q + 1) * over)
    wide = lambda v: jnp.concatenate([v[:, feat:]] * (feat // over), axis=1)
    extra = jnp.where(row == q, top[:, :feat], 0.0)
    extra = jnp.where(row == q + slots, low[:, :feat], extra)
    extra = jnp.where((row == 2 * slots) & mine, wide(top), extra)
    extra = jnp.where((row == 2 * slots + 1) & mine, wide(low), extra)
    extra = extra.astype(jnp.bfloat16)
    tail = pitch - cap_rows - 16
    span = per * pitch - tail
    blank[...] = jnp.zeros(blank.shape, blank.dtype)
    sent = []
    for j in range(3):
        sent.append(
            pltpu.make_async_copy(
                blank, out.at[pl.ds(j * per * pitch + span, tail)], sems.at[11 + j]
            )
        )
        sent[j].start()
    for s in range(4):
        waits[s].wait()
        term = lax.dot_general(sides, w_v[s], NT, preferred_element_type=jnp.float32)
        for k in range(per):
            at = k * pitch
            out_v[s, at : at + cap_rows] = term[:, k * feat : (k + 1) * feat].astype(jnp.bfloat16)
            out_v[s, at + cap_rows : at + cap_rows + 16] = extra
            if k + 1 < per:
                out_v[s, at + cap_rows + 16 : at + pitch] = jnp.zeros((tail, feat), jnp.bfloat16)
        at = pl.multiple_of(slot_of[s] * (per * pitch), 16)
        sent.append(pltpu.make_async_copy(out_v.at[s], out.at[pl.ds(at, span)], sems.at[7 + s]))
        sent[3 + s].start()
    for copy in sent:
        copy.wait()


def term_part(mixed, backs, weights, slot_of, z_index, feat, pitch, out_rows, slots):
    _, cap_rows, ff = mixed.shape
    depth, wide = weights[0].shape
    z_of = jnp.reshape(z_index % slots, (1,)).astype(jnp.int32)
    per = depth // feat
    return pl.pallas_call(
        functools.partial(term_kernel, pitch, slots),
        out_shape=pltpu.HBM((out_rows, feat), jnp.bfloat16),
        in_specs=[SMEM, SMEM] + [HBM] * 6,
        out_specs=HBM,
        scratch_shapes=[
            pltpu.VMEM((3, cap_rows, ff), jnp.float32),
            pltpu.VMEM((4, cap_rows, ff), jnp.bfloat16),
            pltpu.VMEM((4, depth, wide), jnp.bfloat16),
            pltpu.VMEM((4, per * pitch - 16, feat), jnp.bfloat16),
            pltpu.VMEM((16, feat), jnp.bfloat16),
            pltpu.SemaphoreType.DMA((14,)),
        ],
        compiler_params=pltpu.CompilerParams(vmem_limit_bytes=40 << 20),
        cost_estimate=pl.CostEstimate(
            flops=8 * cap_rows * depth * wide, bytes_accessed=14 << 20, transcendentals=0
        ),
    )(slot_of, z_of, mixed, backs, *weights)


def tag_kernel(out_grad, routes, tagged):
    tok_rows, feat = out_grad.shape
    tagged[:tok_rows] = out_grad[...]
    lines = routes[...].astype(jnp.float32)
    lines = jnp.concatenate([lines, jnp.zeros((2, feat - tok_rows), jnp.float32)], axis=1)
    row = lax.broadcasted_iota(jnp.int32, (16, feat), 0)
    tags = jnp.where(row == 0, lines[0:1], jnp.where(row == 1, lines[1:2], 0.0))
    tagged[tok_rows:] = tags.astype(jnp.bfloat16)


def tag(out_grad, routes):
    tok_rows, feat = out_grad.shape
    return pl.pallas_call(
        tag_kernel,
        out_shape=jax.ShapeDtypeStruct((tok_rows + 16, feat), jnp.bfloat16),
        in_specs=[VMEM, VMEM],
        out_specs=VMEM,
        compiler_params=pltpu.CompilerParams(vmem_limit_bytes=8 << 20),
    )(out_grad, routes)


def place_kernel(capacity, routes, tokens, moved_hbm, placed, slot, moved, sem):
    fetch(moved_hbm, moved, sem)
    tok_rows, feat = tokens.shape
    experts = placed.shape[0]
    ids = lax.broadcasted_iota(jnp.int32, (16, tok_rows), 0)
    place_of = lax.broadcasted_iota(jnp.int32, (48, tok_rows), 0)
    before = lax.broadcasted_iota(jnp.int32, (tok_rows, tok_rows), 0) < lax.broadcasted_iota(
        jnp.int32, (tok_rows, tok_rows), 1
    )
    as_ones = lambda mask: jnp.where(mask, 1.0, 0.0).astype(jnp.bfloat16)

    def slots_of(first, second):
        hot = (first == ids) | (second == ids)
        ranks = jnp.dot(as_ones(hot), as_ones(before), preferred_element_type=jnp.float32)
        return [
            jnp.sum(jnp.where(r == ids, ranks, 0.0), axis=0, keepdims=True).astype(jnp.int32)
            for r in (first, second)
        ]

    far = moved[tok_rows:].astype(jnp.float32).astype(jnp.int32)
    kinds = []
    for first, second, rows in (
        (routes[0:1, :], routes[1:2, :], tokens[...]),
        (far[0:1, :tok_rows], far[1:2, :tok_rows], moved[:tok_rows]),
    ):
        kinds.append((first, second, slots_of(first, second), rows))
    slot[...] = jnp.concatenate(kinds[0][2], axis=0)
    for e in range(experts):
        found = []
        for first, second, slots, rows in kinds:
            wanted = jnp.where(first == e, slots[0], jnp.where(second == e, slots[1], -1))
            found.append(
                jnp.dot(as_ones(wanted == place_of), rows, preferred_element_type=jnp.float32)
            )
        placed[e] = jnp.concatenate(found, axis=1)[:capacity].astype(jnp.bfloat16)


def place(routes, tokens, moved, experts, capacity):
    tok_rows, feat = tokens.shape
    vmem = pl.BlockSpec(memory_space=pltpu.VMEM)
    return pl.pallas_call(
        functools.partial(place_kernel, capacity),
        out_shape=(
            jax.ShapeDtypeStruct((experts, capacity, 2 * feat), jnp.bfloat16),
            jax.ShapeDtypeStruct((2, tok_rows), jnp.int32),
        ),
        in_specs=[vmem, vmem, HBM],
        out_specs=(vmem, vmem),
        scratch_shapes=[pltpu.VMEM(moved.shape, moved.dtype), pltpu.SemaphoreType.DMA(())],
        compiler_params=pltpu.CompilerParams(vmem_limit_bytes=8 << 20),
    )(routes, tokens, moved)


def pack_kernel(owners, capacity, slots, z_of, summed, payload, wide):
    feat = summed.shape[1]
    cap_rows = owners * capacity
    over = cap_rows - feat
    count = wide.shape[0]
    wide[pl.ds(0, summed.shape[0]), :] = summed[...].astype(jnp.float32)
    lined = pltpu.roll(wide[...], lax.rem(count - z_of[0], count), 0)
    extra = lined[cap_rows : cap_rows + 16]
    row = lax.broadcasted_iota(jnp.int32, (16, feat), 0)
    lane = lax.broadcasted_iota(jnp.int32, (16, feat), 1)
    head = jnp.sum(jnp.where(row < 2 * slots, extra, 0.0), axis=0, keepdims=True)
    tail = jnp.sum(
        jnp.where((row >= 2 * slots) & (lane < slots * over), extra, 0.0), axis=0, keepdims=True
    )
    tail = sum(tail[:, over * q : over * (q + 1)] for q in range(slots))
    gates = jnp.concatenate([head, tail], axis=1)
    top = gates.astype(jnp.bfloat16).astype(jnp.float32)
    low = gates - top
    blank = jnp.zeros((1, feat - 2 * capacity), jnp.float32)
    rest = jnp.zeros((payload.shape[1] - capacity - 1, feat), jnp.float32)
    for d in range(owners):
        cut = slice(capacity * d, capacity * (d + 1))
        line = jnp.concatenate([top[:, cut], low[:, cut], blank], axis=1)
        rows = lined[capacity * d : capacity * (d + 1)]
        payload[d] = jnp.concatenate([rows, line, rest], axis=0).astype(jnp.bfloat16)


def pack(summed, z_index, owners, capacity, slots, lines):
    rows, feat = summed.shape
    vmem = pl.BlockSpec(memory_space=pltpu.VMEM)
    return pl.pallas_call(
        functools.partial(pack_kernel, owners, capacity, slots),
        out_shape=jax.ShapeDtypeStruct((owners, lines, feat), jnp.bfloat16),
        in_specs=[pl.BlockSpec(memory_space=pltpu.SMEM), vmem],
        out_specs=vmem,
        scratch_shapes=[pltpu.VMEM((rows + 1, feat), jnp.float32)],
    )(jnp.reshape(z_index, (1,)).astype(jnp.int32), summed)


def combine_kernel(capacity, routes, slot, probs, came_hbm, input_grad, gate_grad, came, sem):
    fetch(came_hbm, came, sem)
    tok_rows = routes.shape[1]
    experts, lines, feat = came.shape
    flat = came[...].reshape(experts * lines, feat)
    place_of = lax.broadcasted_iota(jnp.int32, (experts * lines, tok_rows), 0)
    weight = jnp.zeros(place_of.shape, jnp.float32)
    for k in range(2):
        at = routes[k : k + 1, :] * lines + slot[k : k + 1, :]
        weight = jnp.where(place_of == at, probs[k : k + 1, :], weight)
    total = None
    for _ in range(3):
        limb = weight.astype(jnp.bfloat16)
        weight = weight - limb.astype(jnp.float32)
        part = lax.dot_general(
            limb, flat, (((0,), (0,)), ((), ())), preferred_element_type=jnp.float32
        )
        total = part if total is None else total + part
    input_grad[...] = total.astype(jnp.bfloat16)

    gates = jnp.concatenate(
        [came[e, 32:48].astype(jnp.float32)[capacity - 32 : capacity - 31] for e in range(experts)], axis=0
    ).astype(jnp.bfloat16)
    lane_of = lax.broadcasted_iota(jnp.int32, (feat, tok_rows), 0)
    ids = lax.broadcasted_iota(jnp.int32, (experts, tok_rows), 0)
    lines_of = []
    for k in range(2):
        s = slot[k : k + 1, :]
        pick = jnp.where((lane_of == s) | (lane_of == s + capacity), 1.0, 0.0).astype(jnp.bfloat16)
        values = jnp.dot(gates, pick, preferred_element_type=jnp.float32)
        lines_of.append(
            jnp.sum(jnp.where(routes[k : k + 1, :] == ids, values, 0.0), axis=0, keepdims=True)
        )
    gate_grad[...] = jnp.concatenate(lines_of, axis=0)


def combine(routes, slot, probs, came, capacity):
    tok_rows = routes.shape[1]
    feat = came.shape[2]
    vmem = pl.BlockSpec(memory_space=pltpu.VMEM)
    return pl.pallas_call(
        functools.partial(combine_kernel, capacity),
        out_shape=(
            jax.ShapeDtypeStruct((tok_rows, feat), jnp.bfloat16),
            jax.ShapeDtypeStruct((2, tok_rows), jnp.float32),
        ),
        in_specs=[vmem] * 3 + [HBM],
        out_specs=(vmem, vmem),
        scratch_shapes=[pltpu.VMEM(came.shape, came.dtype), pltpu.SemaphoreType.DMA(())],
        compiler_params=pltpu.CompilerParams(vmem_limit_bytes=8 << 20),
    )(routes, slot, probs, came)


def shift(value, axis, step):
    size = lax.axis_size(axis)
    return lax.ppermute(value, axis, [(i, (i + step) % size) for i in range(size)])


def shards(tokens, out_grad, routes, gate_probs, gate_weight, up_weight, down_weight):
    tok_rows, feat = tokens.shape
    owners = lax.axis_size("expert")
    blocks = lax.axis_size("etensor")
    experts = owners * gate_weight.shape[0]
    capacity = min(tok_rows, 9 * tok_rows // (4 * experts))
    x_index = lax.axis_index("dp")
    z_index = lax.axis_index("etensor")
    cap_rows = owners * capacity
    slots = 7

    columns = lax.axis_size("dp")
    gate_up = jnp.concatenate([gate_weight[0], up_weight[0]], axis=1)

    per = blocks // columns
    swap = [
        ((columns * a + w) * columns + x, (columns * x + w) * columns + a)
        for a in range(columns)
        for w in range(per)
        for x in range(columns)
    ]
    moved = lax.ppermute(tag(out_grad, routes.T), ("etensor", "dp"), swap)

    def send():
        placed, slot = place(routes.T, tokens, moved, experts, capacity)
        part = lax.all_to_all(placed, "expert", split_axis=0, concat_axis=0, tiled=True)
        return code(part), slot

    coded, slot = lax.cond(
        x_index >= 0,
        send,
        lambda: (
            jnp.zeros((2 * cap_rows + 16, feat), jnp.int16),
            jnp.zeros((2, tok_rows), jnp.int32),
        ),
    )
    coded = lax.all_gather(coded, "etensor", axis=0, tiled=False)
    coded = pltpu.with_memory_space_constraint(coded, pltpu.HBM)
    backs = lax.all_to_all(
        back_parts(coded, down_weight, cap_rows, columns), "dp", split_axis=0, concat_axis=0, tiled=True
    )

    weights = (gate_up,) + tuple(shift(gate_up, "dp", step) for step in (2, 1, -1))
    slot_of = jnp.stack([(x_index + step) % 4 for step in (0, 2, 3, 1)]).astype(jnp.int32)
    mixed = pltpu.with_memory_space_constraint(
        hidden_part(coded, weights, slot_of, cap_rows), pltpu.HBM
    )
    pitch = cap_rows + 32
    terms = term_part(
        mixed, backs, weights, slot_of, z_index, feat, pitch, blocks * (pitch - 1), slots
    )
    summed = lax.psum_scatter(terms, "etensor", scatter_dimension=0, tiled=True)
    payload = pack(summed, z_index, owners, capacity, slots, 48)
    came = lax.all_to_all(payload, "expert", split_axis=0, concat_axis=0, tiled=True)
    input_grad, gate_grad = combine(routes.T, slot, gate_probs.T, came, capacity)
    return input_grad, gate_grad.T


def solution(mesh):
    return jax.shard_map(
        shards,
        mesh=mesh,
        in_specs=(
            P(("expert", "dp"), "etensor"),
            P(("expert", "dp"), "etensor"),
            P(("expert", "dp"), None),
            P(("expert", "dp"), None),
            P("expert", "dp", "etensor"),
            P("expert", "dp", "etensor"),
            P("expert", "etensor", "dp"),
        ),
        out_specs=(P(("expert", "dp"), "etensor"), P(("expert", "dp"), None)),
        check_vma=False,
    )
```

```python
import functools

import jax
import jax.numpy as jnp
from jax import lax
from jax.experimental import pallas as pl
from jax.experimental.pallas import tpu as pltpu
from jax.sharding import PartitionSpec as P

NT = (((1,), (1,)), ((), ()))


HBM = pl.BlockSpec(memory_space=pltpu.HBM)
VMEM = pl.BlockSpec(memory_space=pltpu.VMEM)
SMEM = pl.BlockSpec(memory_space=pltpu.SMEM)


def fetch(src, dst, sem):
    copy = pltpu.make_async_copy(src, dst, sem)
    copy.start()
    copy.wait()


STEPS = (64, 32, 16, 8, 4, 2, 1)


def code_kernel(rows_hbm, coded, rows, sem):
    fetch(rows_hbm, rows, sem)
    owners, capacity, both = rows.shape
    feat = both // 2
    values = jnp.concatenate([rows[e].astype(jnp.float32) for e in range(owners)], axis=0)
    count = owners * capacity
    tails = []
    for i, half in enumerate((values[:, feat:], values[:, :feat])):
        largest = jnp.max(jnp.max(jnp.abs(half), axis=0, keepdims=True), axis=1, keepdims=True)
        largest = jnp.broadcast_to(largest, (1, feat))
        scale = jnp.ones((1, feat), jnp.float32)
        power = jnp.zeros((1, feat), jnp.int32)
        for step in STEPS:
            fits = largest * (2.0**step) <= 32000.0
            largest = jnp.where(fits, largest * (2.0**step), largest)
            scale = jnp.where(fits, scale * (2.0**step), scale)
            power = jnp.where(fits, power + step, power)
        whole = jnp.round(half * scale).astype(jnp.int32)
        coded[i * count : (i + 1) * count] = whole.astype(jnp.int16)
        tails.append(jnp.broadcast_to(power, (8, feat)))
    coded[2 * count :] = jnp.concatenate(tails, axis=0).astype(jnp.int16)


def code(rows):
    owners, capacity, both = rows.shape
    feat = both // 2
    return pl.pallas_call(
        code_kernel,
        out_shape=jax.ShapeDtypeStruct((2 * owners * capacity + 16, feat), jnp.int16),
        in_specs=[HBM],
        out_specs=VMEM,
        scratch_shapes=[pltpu.VMEM(rows.shape, rows.dtype), pltpu.SemaphoreType.DMA(())],
        compiler_params=pltpu.CompilerParams(vmem_limit_bytes=8 << 20),
    )(rows)


def decode(block, tail, row):
    power = tail.astype(jnp.int32)[row : row + 1]
    scale = jnp.ones(power.shape, jnp.float32)
    for step in STEPS:
        taken = power >= step
        scale = jnp.where(taken, scale * (0.5**step), scale)
        power = jnp.where(taken, power - step, power)
    return (block.astype(jnp.int32).astype(jnp.float32) * scale).astype(jnp.bfloat16)


def back_kernel(coded, down, parts, coded_v, tails_v, down_v, parts_v, sems):
    groups = parts.shape[0]
    per = coded.shape[0] // groups
    cap_rows = parts.shape[1]
    weight = pltpu.make_async_copy(down.at[0], down_v, sems.at[groups])
    tails = pltpu.make_async_copy(
        coded.at[:, pl.ds(2 * cap_rows, 16)], tails_v, sems.at[2 * groups + 1]
    )
    tails.start()
    weight.start()
    copies = [
        pltpu.make_async_copy(
            coded.at[pl.ds(per * g, per), pl.ds(0, cap_rows)], coded_v.at[g], sems.at[g]
        )
        for g in range(groups)
    ]
    for copy in copies:
        copy.start()
    tails.wait()
    weight.wait()
    sent = []
    for g in range(groups):
        copies[g].wait()
        y = jnp.concatenate([decode(coded_v[g, k], tails_v[per * g + k], 0) for k in range(per)], axis=1)
        parts_v[g] = lax.dot_general(y, down_v[...], NT, preferred_element_type=jnp.float32).astype(
            jnp.bfloat16
        )
        sent.append(pltpu.make_async_copy(parts_v.at[g], parts.at[g], sems.at[groups + 1 + g]))
        sent[g].start()
    for copy in sent:
        copy.wait()


def back_parts(coded, down, cap_rows, groups):
    blocks, lines, feat = coded.shape
    _, ff, depth = down.shape
    return pl.pallas_call(
        back_kernel,
        out_shape=pltpu.HBM((groups, cap_rows, ff), jnp.bfloat16),
        in_specs=[HBM, HBM],
        out_specs=HBM,
        scratch_shapes=[
            pltpu.VMEM((groups, blocks // groups, cap_rows, feat), jnp.int16),
            pltpu.VMEM((blocks, 16, feat), jnp.int16),
            pltpu.VMEM((ff, depth), jnp.bfloat16),
            pltpu.VMEM((groups, cap_rows, ff), jnp.bfloat16),
            pltpu.SemaphoreType.DMA((2 * groups + 2,)),
        ],
        compiler_params=pltpu.CompilerParams(vmem_limit_bytes=24 << 20),
        cost_estimate=pl.CostEstimate(
            flops=2 * groups * cap_rows * depth * ff, bytes_accessed=5 << 20, transcendentals=0
        ),
    )(coded, down)


def hidden_kernel(cap_rows, slot_of, coded, *refs):
    weights, (mixed, mixed_v, rows_v, tails_v, w_v, sems) = refs[:4], refs[4:]
    per = coded.shape[0] // 4
    ff = mixed.shape[2]
    waits = []
    for s in range(4):
        blocks = coded.at[pl.ds(slot_of[s] * per, per)]
        rows, tails = blocks.at[:, pl.ds(cap_rows, cap_rows)], blocks.at[:, pl.ds(2 * cap_rows, 16)]
        waits.append(
            [
                pltpu.make_async_copy(tails, tails_v.at[s], sems.at[9 + s]),
                pltpu.make_async_copy(rows, rows_v.at[s], sems.at[2 * s]),
                pltpu.make_async_copy(weights[s], w_v.at[s], sems.at[2 * s + 1]),
            ]
        )
        for copy in waits[s]:
            copy.start()
    total = None
    for s in range(4):
        for copy in waits[s]:
            copy.wait()
        x = jnp.concatenate([decode(rows_v[s, k], tails_v[s, k], 8) for k in range(per)], axis=1)
        part = jnp.dot(x, w_v[s], preferred_element_type=jnp.float32)
        total = part if s == 0 else total + part
    gate_pre, up_pre = total[:, :ff], total[:, ff:]
    sig = 1.0 / (1.0 + jnp.exp(-gate_pre))
    act = gate_pre * sig
    mixed_v[0] = up_pre * sig * (1.0 + gate_pre * (1.0 - sig))
    mixed_v[1] = act
    mixed_v[2] = act * up_pre
    sent = pltpu.make_async_copy(mixed_v, mixed, sems.at[8])
    sent.start()
    sent.wait()


def hidden_part(coded, weights, slot_of, cap_rows):
    blocks, lines, feat = coded.shape
    depth, wide = weights[0].shape
    return pl.pallas_call(
        functools.partial(hidden_kernel, cap_rows),
        out_shape=pltpu.HBM((3, cap_rows, wide // 2), jnp.float32),
        in_specs=[SMEM] + [HBM] * 5,
        out_specs=HBM,
        scratch_shapes=[
            pltpu.VMEM((3, cap_rows, wide // 2), jnp.float32),
            pltpu.VMEM((4, blocks // 4, cap_rows, feat), jnp.int16),
            pltpu.VMEM((4, blocks // 4, 16, feat), jnp.int16),
            pltpu.VMEM((4, depth, wide), jnp.bfloat16),
            pltpu.SemaphoreType.DMA((13,)),
        ],
        compiler_params=pltpu.CompilerParams(vmem_limit_bytes=32 << 20),
        cost_estimate=pl.CostEstimate(
            flops=8 * cap_rows * depth * wide,
            bytes_accessed=12 << 20,
            transcendentals=cap_rows * wide // 2,
        ),
    )(slot_of, coded, *weights)


def term_kernel(pitch, slots, slot_of, z_of, mixed_hbm, backs_hbm, *refs):
    weights, (out, mixed, backs, w_v, out_v, blank, sems) = refs[:4], refs[4:]
    cap_rows = mixed.shape[1]
    feat = out.shape[1]
    per = w_v.shape[1] // feat
    first = [
        pltpu.make_async_copy(backs_hbm, backs, sems.at[4]),
        pltpu.make_async_copy(mixed_hbm, mixed, sems.at[5]),
    ]
    for copy in first:
        copy.start()
    waits = [pltpu.make_async_copy(weights[s], w_v.at[s], sems.at[s]) for s in range(4)]
    for copy in waits:
        copy.start()
    for copy in first:
        copy.wait()
    for s in range(4):
        b = backs[s].astype(jnp.float32)
        back = b if s == 0 else back + b
    prod = mixed[2] * back
    sides = jnp.concatenate(
        [(back * mixed[0]).astype(jnp.bfloat16), (back * mixed[1]).astype(jnp.bfloat16)], axis=1
    )

    ones = jnp.ones((16, prod.shape[1]), jnp.bfloat16)
    total = None
    rest = prod
    for _ in range(3):
        limb = rest.astype(jnp.bfloat16)
        rest = rest - limb.astype(jnp.float32)
        part = lax.dot_general(ones, limb, NT, preferred_element_type=jnp.float32)
        total = part if total is None else total + part
    top = total.astype(jnp.bfloat16).astype(jnp.float32)
    low = total - top
    over = cap_rows - feat
    row = lax.broadcasted_iota(jnp.int32, (16, feat), 0)
    lane = lax.broadcasted_iota(jnp.int32, (16, feat), 1)
    q = z_of[0]
    mine = (lane >= q * over) & (lane < (q + 1) * over)
    wide = lambda v: jnp.concatenate([v[:, feat:]] * (feat // over), axis=1)
    extra = jnp.where(row == q, top[:, :feat], 0.0)
    extra = jnp.where(row == q + slots, low[:, :feat], extra)
    extra = jnp.where((row == 2 * slots) & mine, wide(top), extra)
    extra = jnp.where((row == 2 * slots + 1) & mine, wide(low), extra)
    extra = extra.astype(jnp.bfloat16)
    tail = pitch - cap_rows - 16
    span = per * pitch - tail
    blank[...] = jnp.zeros(blank.shape, blank.dtype)
    sent = []
    for j in range(3):
        sent.append(
            pltpu.make_async_copy(
                blank, out.at[pl.ds(j * per * pitch + span, tail)], sems.at[11 + j]
            )
        )
        sent[j].start()
    for s in range(4):
        waits[s].wait()
        term = lax.dot_general(sides, w_v[s], NT, preferred_element_type=jnp.float32)
        for k in range(per):
            at = k * pitch
            out_v[s, at : at + cap_rows] = term[:, k * feat : (k + 1) * feat].astype(jnp.bfloat16)
            out_v[s, at + cap_rows : at + cap_rows + 16] = extra
            if k + 1 < per:
                out_v[s, at + cap_rows + 16 : at + pitch] = jnp.zeros((tail, feat), jnp.bfloat16)
        at = pl.multiple_of(slot_of[s] * (per * pitch), 16)
        sent.append(pltpu.make_async_copy(out_v.at[s], out.at[pl.ds(at, span)], sems.at[7 + s]))
        sent[3 + s].start()
    for copy in sent:
        copy.wait()


def term_part(mixed, backs, weights, slot_of, z_index, feat, pitch, out_rows, slots):
    _, cap_rows, ff = mixed.shape
    depth, wide = weights[0].shape
    z_of = jnp.reshape(z_index % slots, (1,)).astype(jnp.int32)
    per = depth // feat
    return pl.pallas_call(
        functools.partial(term_kernel, pitch, slots),
        out_shape=pltpu.HBM((out_rows, feat), jnp.bfloat16),
        in_specs=[SMEM, SMEM] + [HBM] * 6,
        out_specs=HBM,
        scratch_shapes=[
            pltpu.VMEM((3, cap_rows, ff), jnp.float32),
            pltpu.VMEM((4, cap_rows, ff), jnp.bfloat16),
            pltpu.VMEM((4, depth, wide), jnp.bfloat16),
            pltpu.VMEM((4, per * pitch - 16, feat), jnp.bfloat16),
            pltpu.VMEM((16, feat), jnp.bfloat16),
            pltpu.SemaphoreType.DMA((14,)),
        ],
        compiler_params=pltpu.CompilerParams(vmem_limit_bytes=40 << 20),
        cost_estimate=pl.CostEstimate(
            flops=8 * cap_rows * depth * wide, bytes_accessed=14 << 20, transcendentals=0
        ),
    )(slot_of, z_of, mixed, backs, *weights)


def tag_kernel(out_grad, routes, tagged):
    tok_rows, feat = out_grad.shape
    tagged[:tok_rows] = out_grad[...]
    lines = routes[...].astype(jnp.float32)
    lines = jnp.concatenate([lines, jnp.zeros((2, feat - tok_rows), jnp.float32)], axis=1)
    row = lax.broadcasted_iota(jnp.int32, (16, feat), 0)
    tags = jnp.where(row == 0, lines[0:1], jnp.where(row == 1, lines[1:2], 0.0))
    tagged[tok_rows:] = tags.astype(jnp.bfloat16)


def tag(out_grad, routes):
    tok_rows, feat = out_grad.shape
    return pl.pallas_call(
        tag_kernel,
        out_shape=jax.ShapeDtypeStruct((tok_rows + 16, feat), jnp.bfloat16),
        in_specs=[VMEM, VMEM],
        out_specs=VMEM,
        compiler_params=pltpu.CompilerParams(vmem_limit_bytes=8 << 20),
    )(out_grad, routes)


def place_kernel(capacity, routes, tokens, moved_hbm, placed, slot, moved, sem):
    fetch(moved_hbm, moved, sem)
    tok_rows, feat = tokens.shape
    experts = placed.shape[0]
    ids = lax.broadcasted_iota(jnp.int32, (16, tok_rows), 0)
    place_of = lax.broadcasted_iota(jnp.int32, (48, tok_rows), 0)
    before = lax.broadcasted_iota(jnp.int32, (tok_rows, tok_rows), 0) < lax.broadcasted_iota(
        jnp.int32, (tok_rows, tok_rows), 1
    )
    as_ones = lambda mask: jnp.where(mask, 1.0, 0.0).astype(jnp.bfloat16)

    def slots_of(first, second):
        hot = (first == ids) | (second == ids)
        ranks = jnp.dot(as_ones(hot), as_ones(before), preferred_element_type=jnp.float32)
        return [
            jnp.sum(jnp.where(r == ids, ranks, 0.0), axis=0, keepdims=True).astype(jnp.int32)
            for r in (first, second)
        ]

    far = moved[tok_rows:].astype(jnp.float32).astype(jnp.int32)
    kinds = []
    for first, second, rows in (
        (routes[0:1, :], routes[1:2, :], tokens[...]),
        (far[0:1, :tok_rows], far[1:2, :tok_rows], moved[:tok_rows]),
    ):
        kinds.append((first, second, slots_of(first, second), rows))
    slot[...] = jnp.concatenate(kinds[0][2], axis=0)
    for e in range(experts):
        found = []
        for first, second, slots, rows in kinds:
            wanted = jnp.where(first == e, slots[0], jnp.where(second == e, slots[1], -1))
            found.append(
                jnp.dot(as_ones(wanted == place_of), rows, preferred_element_type=jnp.float32)
            )
        placed[e] = jnp.concatenate(found, axis=1)[:capacity].astype(jnp.bfloat16)


def place(routes, tokens, moved, experts, capacity):
    tok_rows, feat = tokens.shape
    vmem = pl.BlockSpec(memory_space=pltpu.VMEM)
    return pl.pallas_call(
        functools.partial(place_kernel, capacity),
        out_shape=(
            jax.ShapeDtypeStruct((experts, capacity, 2 * feat), jnp.bfloat16),
            jax.ShapeDtypeStruct((2, tok_rows), jnp.int32),
        ),
        in_specs=[vmem, vmem, HBM],
        out_specs=(vmem, vmem),
        scratch_shapes=[pltpu.VMEM(moved.shape, moved.dtype), pltpu.SemaphoreType.DMA(())],
        compiler_params=pltpu.CompilerParams(vmem_limit_bytes=8 << 20),
    )(routes, tokens, moved)


def pack_kernel(owners, capacity, slots, z_of, summed, payload, wide):
    feat = summed.shape[1]
    cap_rows = owners * capacity
    over = cap_rows - feat
    count = wide.shape[0]
    wide[pl.ds(0, summed.shape[0]), :] = summed[...].astype(jnp.float32)
    lined = pltpu.roll(wide[...], lax.rem(count - z_of[0], count), 0)
    extra = lined[cap_rows : cap_rows + 16]
    row = lax.broadcasted_iota(jnp.int32, (16, feat), 0)
    lane = lax.broadcasted_iota(jnp.int32, (16, feat), 1)
    head = jnp.sum(jnp.where(row < 2 * slots, extra, 0.0), axis=0, keepdims=True)
    tail = jnp.sum(
        jnp.where((row >= 2 * slots) & (lane < slots * over), extra, 0.0), axis=0, keepdims=True
    )
    tail = sum(tail[:, over * q : over * (q + 1)] for q in range(slots))
    gates = jnp.concatenate([head, tail], axis=1)
    top = gates.astype(jnp.bfloat16).astype(jnp.float32)
    low = gates - top
    blank = jnp.zeros((1, feat - 2 * capacity), jnp.float32)
    rest = jnp.zeros((payload.shape[1] - capacity - 1, feat), jnp.float32)
    for d in range(owners):
        cut = slice(capacity * d, capacity * (d + 1))
        line = jnp.concatenate([top[:, cut], low[:, cut], blank], axis=1)
        rows = lined[capacity * d : capacity * (d + 1)]
        payload[d] = jnp.concatenate([rows, line, rest], axis=0).astype(jnp.bfloat16)


def pack(summed, z_index, owners, capacity, slots, lines):
    rows, feat = summed.shape
    vmem = pl.BlockSpec(memory_space=pltpu.VMEM)
    return pl.pallas_call(
        functools.partial(pack_kernel, owners, capacity, slots),
        out_shape=jax.ShapeDtypeStruct((owners, lines, feat), jnp.bfloat16),
        in_specs=[pl.BlockSpec(memory_space=pltpu.SMEM), vmem],
        out_specs=vmem,
        scratch_shapes=[pltpu.VMEM((rows + 1, feat), jnp.float32)],
    )(jnp.reshape(z_index, (1,)).astype(jnp.int32), summed)


def combine_kernel(capacity, routes, slot, probs, came_hbm, input_grad, gate_grad, came, sem):
    fetch(came_hbm, came, sem)
    tok_rows = routes.shape[1]
    experts, lines, feat = came.shape
    flat = came[...].reshape(experts * lines, feat)
    place_of = lax.broadcasted_iota(jnp.int32, (experts * lines, tok_rows), 0)
    weight = jnp.zeros(place_of.shape, jnp.float32)
    for k in range(2):
        at = routes[k : k + 1, :] * lines + slot[k : k + 1, :]
        weight = jnp.where(place_of == at, probs[k : k + 1, :], weight)
    total = None
    for _ in range(3):
        limb = weight.astype(jnp.bfloat16)
        weight = weight - limb.astype(jnp.float32)
        part = lax.dot_general(
            limb, flat, (((0,), (0,)), ((), ())), preferred_element_type=jnp.float32
        )
        total = part if total is None else total + part
    input_grad[...] = total.astype(jnp.bfloat16)

    gates = jnp.concatenate(
        [came[e, 32:48].astype(jnp.float32)[capacity - 32 : capacity - 31] for e in range(experts)], axis=0
    ).astype(jnp.bfloat16)
    lane_of = lax.broadcasted_iota(jnp.int32, (feat, tok_rows), 0)
    ids = lax.broadcasted_iota(jnp.int32, (experts, tok_rows), 0)
    lines_of = []
    for k in range(2):
        s = slot[k : k + 1, :]
        pick = jnp.where((lane_of == s) | (lane_of == s + capacity), 1.0, 0.0).astype(jnp.bfloat16)
        values = jnp.dot(gates, pick, preferred_element_type=jnp.float32)
        lines_of.append(
            jnp.sum(jnp.where(routes[k : k + 1, :] == ids, values, 0.0), axis=0, keepdims=True)
        )
    gate_grad[...] = jnp.concatenate(lines_of, axis=0)


def combine(routes, slot, probs, came, capacity):
    tok_rows = routes.shape[1]
    feat = came.shape[2]
    vmem = pl.BlockSpec(memory_space=pltpu.VMEM)
    return pl.pallas_call(
        functools.partial(combine_kernel, capacity),
        out_shape=(
            jax.ShapeDtypeStruct((tok_rows, feat), jnp.bfloat16),
            jax.ShapeDtypeStruct((2, tok_rows), jnp.float32),
        ),
        in_specs=[vmem] * 3 + [HBM],
        out_specs=(vmem, vmem),
        scratch_shapes=[pltpu.VMEM(came.shape, came.dtype), pltpu.SemaphoreType.DMA(())],
        compiler_params=pltpu.CompilerParams(vmem_limit_bytes=8 << 20),
    )(routes, slot, probs, came)


def trade(value, axis, bits):
    return lax.ppermute(value, axis, [(i, i ^ bits) for i in range(lax.axis_size(axis))])


def shards(tokens, out_grad, routes, gate_probs, gate_weight, up_weight, down_weight):
    tok_rows, feat = tokens.shape
    owners = lax.axis_size("expert")
    blocks = lax.axis_size("etensor")
    experts = owners * gate_weight.shape[0]
    capacity = min(tok_rows, 9 * tok_rows // (4 * experts))
    x_index = lax.axis_index("dp")
    z_index = lax.axis_index("etensor")
    cap_rows = owners * capacity
    slots = 7

    columns = lax.axis_size("dp")
    gate_up = jnp.concatenate([gate_weight[0], up_weight[0]], axis=1)

    per = blocks // columns
    swap = [
        ((columns * a + w) * columns + x, (columns * x + w) * columns + a)
        for a in range(columns)
        for w in range(per)
        for x in range(columns)
    ]
    moved = lax.ppermute(tag(out_grad, routes.T), ("etensor", "dp"), swap)

    def send():
        placed, slot = place(routes.T, tokens, moved, experts, capacity)
        part = lax.all_to_all(placed, "expert", split_axis=0, concat_axis=0, tiled=True)
        return code(part), slot

    coded, slot = lax.cond(
        x_index >= 0,
        send,
        lambda: (
            jnp.zeros((2 * cap_rows + 16, feat), jnp.int16),
            jnp.zeros((2, tok_rows), jnp.int32),
        ),
    )
    coded = lax.all_gather(coded, "etensor", axis=0, tiled=False)
    coded = pltpu.with_memory_space_constraint(coded, pltpu.HBM)
    backs = lax.all_to_all(
        back_parts(coded, down_weight, cap_rows, columns), "dp", split_axis=0, concat_axis=0, tiled=True
    )

    weights = (gate_up,) + tuple(trade(gate_up, "dp", bits) for bits in (2, 1, 3))
    slot_of = jnp.stack([x_index ^ bits for bits in (0, 2, 1, 3)]).astype(jnp.int32)
    mixed = pltpu.with_memory_space_constraint(
        hidden_part(coded, weights, slot_of, cap_rows), pltpu.HBM
    )
    pitch = cap_rows + 32
    terms = term_part(
        mixed, backs, weights, slot_of, z_index, feat, pitch, blocks * (pitch - 1), slots
    )
    summed = lax.psum_scatter(terms, "etensor", scatter_dimension=0, tiled=True)
    payload = pack(summed, z_index, owners, capacity, slots, 48)
    came = lax.all_to_all(payload, "expert", split_axis=0, concat_axis=0, tiled=True)
    input_grad, gate_grad = combine(routes.T, slot, gate_probs.T, came, capacity)
    return input_grad, gate_grad.T


def solution(mesh):
    return jax.shard_map(
        shards,
        mesh=mesh,
        in_specs=(
            P(("expert", "dp"), "etensor"),
            P(("expert", "dp"), "etensor"),
            P(("expert", "dp"), None),
            P(("expert", "dp"), None),
            P("expert", "dp", "etensor"),
            P("expert", "dp", "etensor"),
            P("expert", "etensor", "dp"),
        ),
        out_specs=(P(("expert", "dp"), "etensor"), P(("expert", "dp"), None)),
        check_vma=False,
    )
```

```python
import functools

import jax
import jax.numpy as jnp
from jax import lax
from jax.experimental import pallas as pl
from jax.experimental.pallas import tpu as pltpu
from jax.sharding import PartitionSpec as P

NT = (((1,), (1,)), ((), ()))


HBM = pl.BlockSpec(memory_space=pltpu.HBM)
VMEM = pl.BlockSpec(memory_space=pltpu.VMEM)
SMEM = pl.BlockSpec(memory_space=pltpu.SMEM)


def fetch(src, dst, sem):
    copy = pltpu.make_async_copy(src, dst, sem)
    copy.start()
    copy.wait()


STEPS = (64, 32, 16, 8, 4, 2, 1)


def code_kernel(rows_hbm, coded, rows, sem):
    fetch(rows_hbm, rows, sem)
    owners, capacity, both = rows.shape
    feat = both // 2
    values = jnp.concatenate([rows[e].astype(jnp.float32) for e in range(owners)], axis=0)
    count = owners * capacity
    tails = []
    for i, half in enumerate((values[:, feat:], values[:, :feat])):
        largest = jnp.max(jnp.max(jnp.abs(half), axis=0, keepdims=True), axis=1, keepdims=True)
        largest = jnp.broadcast_to(largest, (1, feat))
        scale = jnp.ones((1, feat), jnp.float32)
        power = jnp.zeros((1, feat), jnp.int32)
        for step in STEPS:
            fits = largest * (2.0**step) <= 32000.0
            largest = jnp.where(fits, largest * (2.0**step), largest)
            scale = jnp.where(fits, scale * (2.0**step), scale)
            power = jnp.where(fits, power + step, power)
        whole = jnp.round(half * scale).astype(jnp.int32)
        coded[i * count : (i + 1) * count] = whole.astype(jnp.int16)
        tails.append(jnp.broadcast_to(power, (8, feat)))
    coded[2 * count :] = jnp.concatenate(tails, axis=0).astype(jnp.int16)


def code(rows):
    owners, capacity, both = rows.shape
    feat = both // 2
    return pl.pallas_call(
        code_kernel,
        out_shape=jax.ShapeDtypeStruct((2 * owners * capacity + 16, feat), jnp.int16),
        in_specs=[HBM],
        out_specs=VMEM,
        scratch_shapes=[pltpu.VMEM(rows.shape, rows.dtype), pltpu.SemaphoreType.DMA(())],
        compiler_params=pltpu.CompilerParams(vmem_limit_bytes=8 << 20),
    )(rows)


def decode(block, tail, row):
    power = tail.astype(jnp.int32)[row : row + 1]
    scale = jnp.ones(power.shape, jnp.float32)
    for step in STEPS:
        taken = power >= step
        scale = jnp.where(taken, scale * (0.5**step), scale)
        power = jnp.where(taken, power - step, power)
    return (block.astype(jnp.int32).astype(jnp.float32) * scale).astype(jnp.bfloat16)


def back_kernel(coded, down, parts, coded_v, tails_v, down_v, parts_v, sems):
    groups = parts.shape[0]
    per = coded.shape[0] // groups
    cap_rows = parts.shape[1]
    weight = pltpu.make_async_copy(down.at[0], down_v, sems.at[groups])
    tails = pltpu.make_async_copy(
        coded.at[:, pl.ds(2 * cap_rows, 16)], tails_v, sems.at[2 * groups + 1]
    )
    tails.start()
    weight.start()
    copies = [
        pltpu.make_async_copy(
            coded.at[pl.ds(per * g, per), pl.ds(0, cap_rows)], coded_v.at[g], sems.at[g]
        )
        for g in range(groups)
    ]
    for copy in copies:
        copy.start()
    tails.wait()
    weight.wait()
    sent = []
    for g in range(groups):
        copies[g].wait()
        y = jnp.concatenate([decode(coded_v[g, k], tails_v[per * g + k], 0) for k in range(per)], axis=1)
        parts_v[g] = lax.dot_general(y, down_v[...], NT, preferred_element_type=jnp.float32).astype(
            jnp.bfloat16
        )
        sent.append(pltpu.make_async_copy(parts_v.at[g], parts.at[g], sems.at[groups + 1 + g]))
        sent[g].start()
    for copy in sent:
        copy.wait()


def back_parts(coded, down, cap_rows, groups):
    blocks, lines, feat = coded.shape
    _, ff, depth = down.shape
    return pl.pallas_call(
        back_kernel,
        out_shape=pltpu.HBM((groups, cap_rows, ff), jnp.bfloat16),
        in_specs=[HBM, HBM],
        out_specs=HBM,
        scratch_shapes=[
            pltpu.VMEM((groups, blocks // groups, cap_rows, feat), jnp.int16),
            pltpu.VMEM((blocks, 16, feat), jnp.int16),
            pltpu.VMEM((ff, depth), jnp.bfloat16),
            pltpu.VMEM((groups, cap_rows, ff), jnp.bfloat16),
            pltpu.SemaphoreType.DMA((2 * groups + 2,)),
        ],
        compiler_params=pltpu.CompilerParams(vmem_limit_bytes=24 << 20),
        cost_estimate=pl.CostEstimate(
            flops=2 * groups * cap_rows * depth * ff, bytes_accessed=5 << 20, transcendentals=0
        ),
    )(coded, down)


def hidden_kernel(cap_rows, slot_of, coded, *refs):
    weights, (mixed, mixed_v, rows_v, tails_v, w_v, sems) = refs[:4], refs[4:]
    per = coded.shape[0] // 4
    ff = mixed.shape[2]
    waits = []
    for s in range(4):
        blocks = coded.at[pl.ds(slot_of[s] * per, per)]
        rows, tails = blocks.at[:, pl.ds(cap_rows, cap_rows)], blocks.at[:, pl.ds(2 * cap_rows, 16)]
        waits.append(
            [
                pltpu.make_async_copy(tails, tails_v.at[s], sems.at[9 + s]),
                pltpu.make_async_copy(rows, rows_v.at[s], sems.at[2 * s]),
                pltpu.make_async_copy(weights[s], w_v.at[s], sems.at[2 * s + 1]),
            ]
        )
        for copy in waits[s]:
            copy.start()
    total = None
    for s in range(4):
        for copy in waits[s]:
            copy.wait()
        x = jnp.concatenate([decode(rows_v[s, k], tails_v[s, k], 8) for k in range(per)], axis=1)
        part = jnp.dot(x, w_v[s], preferred_element_type=jnp.float32)
        total = part if s == 0 else total + part
    gate_pre, up_pre = total[:, :ff], total[:, ff:]
    sig = 1.0 / (1.0 + jnp.exp(-gate_pre))
    act = gate_pre * sig
    mixed_v[0] = up_pre * sig * (1.0 + gate_pre * (1.0 - sig))
    mixed_v[1] = act
    mixed_v[2] = act * up_pre
    sent = pltpu.make_async_copy(mixed_v, mixed, sems.at[8])
    sent.start()
    sent.wait()


def hidden_part(coded, weights, slot_of, cap_rows):
    blocks, lines, feat = coded.shape
    depth, wide = weights[0].shape
    return pl.pallas_call(
        functools.partial(hidden_kernel, cap_rows),
        out_shape=pltpu.HBM((3, cap_rows, wide // 2), jnp.float32),
        in_specs=[SMEM] + [HBM] * 5,
        out_specs=HBM,
        scratch_shapes=[
            pltpu.VMEM((3, cap_rows, wide // 2), jnp.float32),
            pltpu.VMEM((4, blocks // 4, cap_rows, feat), jnp.int16),
            pltpu.VMEM((4, blocks // 4, 16, feat), jnp.int16),
            pltpu.VMEM((4, depth, wide), jnp.bfloat16),
            pltpu.SemaphoreType.DMA((13,)),
        ],
        compiler_params=pltpu.CompilerParams(vmem_limit_bytes=32 << 20),
        cost_estimate=pl.CostEstimate(
            flops=8 * cap_rows * depth * wide,
            bytes_accessed=12 << 20,
            transcendentals=cap_rows * wide // 2,
        ),
    )(slot_of, coded, *weights)


def term_kernel(pitch, slots, slot_of, z_of, mixed_hbm, backs_hbm, *refs):
    weights, (out, mixed, backs, w_v, out_v, blank, sems) = refs[:4], refs[4:]
    cap_rows = mixed.shape[1]
    feat = out.shape[1]
    per = w_v.shape[1] // feat
    first = [
        pltpu.make_async_copy(backs_hbm, backs, sems.at[4]),
        pltpu.make_async_copy(mixed_hbm, mixed, sems.at[5]),
    ]
    for copy in first:
        copy.start()
    waits = [pltpu.make_async_copy(weights[s], w_v.at[s], sems.at[s]) for s in range(4)]
    for copy in waits:
        copy.start()
    for copy in first:
        copy.wait()
    for s in range(4):
        b = backs[s].astype(jnp.float32)
        back = b if s == 0 else back + b
    prod = mixed[2] * back
    sides = jnp.concatenate(
        [(back * mixed[0]).astype(jnp.bfloat16), (back * mixed[1]).astype(jnp.bfloat16)], axis=1
    )

    prod = sum(prod[:, 128 * i : 128 * (i + 1)] for i in range(prod.shape[1] // 128))
    ones = jnp.ones((16, prod.shape[1]), jnp.bfloat16)
    total = None
    rest = prod
    for _ in range(3):
        limb = rest.astype(jnp.bfloat16)
        rest = rest - limb.astype(jnp.float32)
        part = lax.dot_general(ones, limb, NT, preferred_element_type=jnp.float32)
        total = part if total is None else total + part
    top = total.astype(jnp.bfloat16).astype(jnp.float32)
    low = total - top
    over = cap_rows - feat
    row = lax.broadcasted_iota(jnp.int32, (16, feat), 0)
    lane = lax.broadcasted_iota(jnp.int32, (16, feat), 1)
    q = z_of[0]
    mine = (lane >= q * over) & (lane < (q + 1) * over)
    wide = lambda v: jnp.concatenate([v[:, feat:]] * (feat // over), axis=1)
    extra = jnp.where(row == q, top[:, :feat], 0.0)
    extra = jnp.where(row == q + slots, low[:, :feat], extra)
    extra = jnp.where((row == 2 * slots) & mine, wide(top), extra)
    extra = jnp.where((row == 2 * slots + 1) & mine, wide(low), extra)
    extra = extra.astype(jnp.bfloat16)
    tail = pitch - cap_rows - 16
    span = per * pitch - tail
    blank[...] = jnp.zeros(blank.shape, blank.dtype)
    sent = []
    for j in range(3):
        sent.append(
            pltpu.make_async_copy(
                blank, out.at[pl.ds(j * per * pitch + span, tail)], sems.at[11 + j]
            )
        )
        sent[j].start()
    for s in range(4):
        waits[s].wait()
        term = lax.dot_general(sides, w_v[s], NT, preferred_element_type=jnp.float32)
        for k in range(per):
            at = k * pitch
            out_v[s, at : at + cap_rows] = term[:, k * feat : (k + 1) * feat].astype(jnp.bfloat16)
            out_v[s, at + cap_rows : at + cap_rows + 16] = extra
            if k + 1 < per:
                out_v[s, at + cap_rows + 16 : at + pitch] = jnp.zeros((tail, feat), jnp.bfloat16)
        at = pl.multiple_of(slot_of[s] * (per * pitch), 16)
        sent.append(pltpu.make_async_copy(out_v.at[s], out.at[pl.ds(at, span)], sems.at[7 + s]))
        sent[3 + s].start()
    for copy in sent:
        copy.wait()


def term_part(mixed, backs, weights, slot_of, z_index, feat, pitch, out_rows, slots):
    _, cap_rows, ff = mixed.shape
    depth, wide = weights[0].shape
    z_of = jnp.reshape(z_index % slots, (1,)).astype(jnp.int32)
    per = depth // feat
    return pl.pallas_call(
        functools.partial(term_kernel, pitch, slots),
        out_shape=pltpu.HBM((out_rows, feat), jnp.bfloat16),
        in_specs=[SMEM, SMEM] + [HBM] * 6,
        out_specs=HBM,
        scratch_shapes=[
            pltpu.VMEM((3, cap_rows, ff), jnp.float32),
            pltpu.VMEM((4, cap_rows, ff), jnp.bfloat16),
            pltpu.VMEM((4, depth, wide), jnp.bfloat16),
            pltpu.VMEM((4, per * pitch - 16, feat), jnp.bfloat16),
            pltpu.VMEM((16, feat), jnp.bfloat16),
            pltpu.SemaphoreType.DMA((14,)),
        ],
        compiler_params=pltpu.CompilerParams(vmem_limit_bytes=40 << 20),
        cost_estimate=pl.CostEstimate(
            flops=8 * cap_rows * depth * wide, bytes_accessed=14 << 20, transcendentals=0
        ),
    )(slot_of, z_of, mixed, backs, *weights)


def tag_kernel(out_grad, routes, tagged):
    tok_rows, feat = out_grad.shape
    tagged[:tok_rows] = out_grad[...]
    lines = routes[...].astype(jnp.float32)
    lines = jnp.concatenate([lines, jnp.zeros((2, feat - tok_rows), jnp.float32)], axis=1)
    row = lax.broadcasted_iota(jnp.int32, (16, feat), 0)
    tags = jnp.where(row == 0, lines[0:1], jnp.where(row == 1, lines[1:2], 0.0))
    tagged[tok_rows:] = tags.astype(jnp.bfloat16)


def tag(out_grad, routes):
    tok_rows, feat = out_grad.shape
    return pl.pallas_call(
        tag_kernel,
        out_shape=jax.ShapeDtypeStruct((tok_rows + 16, feat), jnp.bfloat16),
        in_specs=[VMEM, VMEM],
        out_specs=VMEM,
        compiler_params=pltpu.CompilerParams(vmem_limit_bytes=8 << 20),
    )(out_grad, routes)


def place_kernel(capacity, routes, tokens, moved_hbm, placed, slot, moved, sem):
    fetch(moved_hbm, moved, sem)
    tok_rows, feat = tokens.shape
    experts = placed.shape[0]
    ids = lax.broadcasted_iota(jnp.int32, (16, tok_rows), 0)
    place_of = lax.broadcasted_iota(jnp.int32, (48, tok_rows), 0)
    before = lax.broadcasted_iota(jnp.int32, (tok_rows, tok_rows), 0) < lax.broadcasted_iota(
        jnp.int32, (tok_rows, tok_rows), 1
    )
    as_ones = lambda mask: jnp.where(mask, 1.0, 0.0).astype(jnp.bfloat16)

    def slots_of(first, second):
        hot = (first == ids) | (second == ids)
        ranks = jnp.dot(as_ones(hot), as_ones(before), preferred_element_type=jnp.float32)
        return [
            jnp.sum(jnp.where(r == ids, ranks, 0.0), axis=0, keepdims=True).astype(jnp.int32)
            for r in (first, second)
        ]

    far = moved[tok_rows:].astype(jnp.float32).astype(jnp.int32)
    kinds = []
    for first, second, rows in (
        (routes[0:1, :], routes[1:2, :], tokens[...]),
        (far[0:1, :tok_rows], far[1:2, :tok_rows], moved[:tok_rows]),
    ):
        kinds.append((first, second, slots_of(first, second), rows))
    slot[...] = jnp.concatenate(kinds[0][2], axis=0)
    for e in range(experts):
        found = []
        for first, second, slots, rows in kinds:
            wanted = jnp.where(first == e, slots[0], jnp.where(second == e, slots[1], -1))
            found.append(
                jnp.dot(as_ones(wanted == place_of), rows, preferred_element_type=jnp.float32)
            )
        placed[e] = jnp.concatenate(found, axis=1)[:capacity].astype(jnp.bfloat16)


def place(routes, tokens, moved, experts, capacity):
    tok_rows, feat = tokens.shape
    vmem = pl.BlockSpec(memory_space=pltpu.VMEM)
    return pl.pallas_call(
        functools.partial(place_kernel, capacity),
        out_shape=(
            jax.ShapeDtypeStruct((experts, capacity, 2 * feat), jnp.bfloat16),
            jax.ShapeDtypeStruct((2, tok_rows), jnp.int32),
        ),
        in_specs=[vmem, vmem, HBM],
        out_specs=(vmem, vmem),
        scratch_shapes=[pltpu.VMEM(moved.shape, moved.dtype), pltpu.SemaphoreType.DMA(())],
        compiler_params=pltpu.CompilerParams(vmem_limit_bytes=8 << 20),
    )(routes, tokens, moved)


def pack_kernel(owners, capacity, slots, z_of, summed, payload, wide):
    feat = summed.shape[1]
    cap_rows = owners * capacity
    over = cap_rows - feat
    count = wide.shape[0]
    wide[pl.ds(0, summed.shape[0]), :] = summed[...].astype(jnp.float32)
    lined = pltpu.roll(wide[...], lax.rem(count - z_of[0], count), 0)
    extra = lined[cap_rows : cap_rows + 16]
    row = lax.broadcasted_iota(jnp.int32, (16, feat), 0)
    lane = lax.broadcasted_iota(jnp.int32, (16, feat), 1)
    head = jnp.sum(jnp.where(row < 2 * slots, extra, 0.0), axis=0, keepdims=True)
    tail = jnp.sum(
        jnp.where((row >= 2 * slots) & (lane < slots * over), extra, 0.0), axis=0, keepdims=True
    )
    tail = sum(tail[:, over * q : over * (q + 1)] for q in range(slots))
    gates = jnp.concatenate([head, tail], axis=1)
    top = gates.astype(jnp.bfloat16).astype(jnp.float32)
    low = gates - top
    blank = jnp.zeros((1, feat - 2 * capacity), jnp.float32)
    rest = jnp.zeros((payload.shape[1] - capacity - 1, feat), jnp.float32)
    for d in range(owners):
        cut = slice(capacity * d, capacity * (d + 1))
        line = jnp.concatenate([top[:, cut], low[:, cut], blank], axis=1)
        rows = lined[capacity * d : capacity * (d + 1)]
        payload[d] = jnp.concatenate([rows, line, rest], axis=0).astype(jnp.bfloat16)


def pack(summed, z_index, owners, capacity, slots, lines):
    rows, feat = summed.shape
    vmem = pl.BlockSpec(memory_space=pltpu.VMEM)
    return pl.pallas_call(
        functools.partial(pack_kernel, owners, capacity, slots),
        out_shape=jax.ShapeDtypeStruct((owners, lines, feat), jnp.bfloat16),
        in_specs=[pl.BlockSpec(memory_space=pltpu.SMEM), vmem],
        out_specs=vmem,
        scratch_shapes=[pltpu.VMEM((rows + 1, feat), jnp.float32)],
    )(jnp.reshape(z_index, (1,)).astype(jnp.int32), summed)


def combine_kernel(capacity, routes, slot, probs, came_hbm, input_grad, gate_grad, came, sem):
    fetch(came_hbm, came, sem)
    tok_rows = routes.shape[1]
    experts, lines, feat = came.shape
    flat = came[...].reshape(experts * lines, feat)
    place_of = lax.broadcasted_iota(jnp.int32, (experts * lines, tok_rows), 0)
    weight = jnp.zeros(place_of.shape, jnp.float32)
    for k in range(2):
        at = routes[k : k + 1, :] * lines + slot[k : k + 1, :]
        weight = jnp.where(place_of == at, probs[k : k + 1, :], weight)
    total = None
    for _ in range(3):
        limb = weight.astype(jnp.bfloat16)
        weight = weight - limb.astype(jnp.float32)
        part = lax.dot_general(
            limb, flat, (((0,), (0,)), ((), ())), preferred_element_type=jnp.float32
        )
        total = part if total is None else total + part
    input_grad[...] = total.astype(jnp.bfloat16)

    gates = jnp.concatenate(
        [came[e, 32:48].astype(jnp.float32)[capacity - 32 : capacity - 31] for e in range(experts)], axis=0
    ).astype(jnp.bfloat16)
    lane_of = lax.broadcasted_iota(jnp.int32, (feat, tok_rows), 0)
    ids = lax.broadcasted_iota(jnp.int32, (experts, tok_rows), 0)
    lines_of = []
    for k in range(2):
        s = slot[k : k + 1, :]
        pick = jnp.where((lane_of == s) | (lane_of == s + capacity), 1.0, 0.0).astype(jnp.bfloat16)
        values = jnp.dot(gates, pick, preferred_element_type=jnp.float32)
        lines_of.append(
            jnp.sum(jnp.where(routes[k : k + 1, :] == ids, values, 0.0), axis=0, keepdims=True)
        )
    gate_grad[...] = jnp.concatenate(lines_of, axis=0)


def combine(routes, slot, probs, came, capacity):
    tok_rows = routes.shape[1]
    feat = came.shape[2]
    vmem = pl.BlockSpec(memory_space=pltpu.VMEM)
    return pl.pallas_call(
        functools.partial(combine_kernel, capacity),
        out_shape=(
            jax.ShapeDtypeStruct((tok_rows, feat), jnp.bfloat16),
            jax.ShapeDtypeStruct((2, tok_rows), jnp.float32),
        ),
        in_specs=[vmem] * 3 + [HBM],
        out_specs=(vmem, vmem),
        scratch_shapes=[pltpu.VMEM(came.shape, came.dtype), pltpu.SemaphoreType.DMA(())],
        compiler_params=pltpu.CompilerParams(vmem_limit_bytes=8 << 20),
    )(routes, slot, probs, came)


def trade(value, axis, bits):
    return lax.ppermute(value, axis, [(i, i ^ bits) for i in range(lax.axis_size(axis))])


def shards(tokens, out_grad, routes, gate_probs, gate_weight, up_weight, down_weight):
    tok_rows, feat = tokens.shape
    owners = lax.axis_size("expert")
    blocks = lax.axis_size("etensor")
    experts = owners * gate_weight.shape[0]
    capacity = min(tok_rows, 9 * tok_rows // (4 * experts))
    x_index = lax.axis_index("dp")
    z_index = lax.axis_index("etensor")
    cap_rows = owners * capacity
    slots = 7

    columns = lax.axis_size("dp")
    gate_up = jnp.concatenate([gate_weight[0], up_weight[0]], axis=1)

    per = blocks // columns
    swap = [
        ((columns * a + w) * columns + x, (columns * x + w) * columns + a)
        for a in range(columns)
        for w in range(per)
        for x in range(columns)
    ]
    moved = lax.ppermute(tag(out_grad, routes.T), ("etensor", "dp"), swap)

    def send():
        placed, slot = place(routes.T, tokens, moved, experts, capacity)
        part = lax.all_to_all(placed, "expert", split_axis=0, concat_axis=0, tiled=True)
        return code(part), slot

    coded, slot = lax.cond(
        x_index >= 0,
        send,
        lambda: (
            jnp.zeros((2 * cap_rows + 16, feat), jnp.int16),
            jnp.zeros((2, tok_rows), jnp.int32),
        ),
    )
    coded = lax.all_gather(coded, "etensor", axis=0, tiled=False)
    coded = pltpu.with_memory_space_constraint(coded, pltpu.HBM)
    backs = lax.all_to_all(
        back_parts(coded, down_weight, cap_rows, columns), "dp", split_axis=0, concat_axis=0, tiled=True
    )

    weights = (gate_up,) + tuple(trade(gate_up, "dp", bits) for bits in (2, 1, 3))
    slot_of = jnp.stack([x_index ^ bits for bits in (0, 2, 1, 3)]).astype(jnp.int32)
    mixed = pltpu.with_memory_space_constraint(
        hidden_part(coded, weights, slot_of, cap_rows), pltpu.HBM
    )
    pitch = cap_rows + 32
    terms = term_part(
        mixed, backs, weights, slot_of, z_index, feat, pitch, blocks * (pitch - 1), slots
    )
    summed = lax.psum_scatter(terms, "etensor", scatter_dimension=0, tiled=True)
    payload = pack(summed, z_index, owners, capacity, slots, 48)
    came = lax.all_to_all(payload, "expert", split_axis=0, concat_axis=0, tiled=True)
    input_grad, gate_grad = combine(routes.T, slot, gate_probs.T, came, capacity)
    return input_grad, gate_grad.T


def solution(mesh):
    return jax.shard_map(
        shards,
        mesh=mesh,
        in_specs=(
            P(("expert", "dp"), "etensor"),
            P(("expert", "dp"), "etensor"),
            P(("expert", "dp"), None),
            P(("expert", "dp"), None),
            P("expert", "dp", "etensor"),
            P("expert", "dp", "etensor"),
            P("expert", "etensor", "dp"),
        ),
        out_specs=(P(("expert", "dp"), "etensor"), P(("expert", "dp"), None)),
        check_vma=False,
    )
```

```python
import functools

import jax
import jax.numpy as jnp
from jax import lax
from jax.experimental import pallas as pl
from jax.experimental.pallas import tpu as pltpu
from jax.sharding import PartitionSpec as P

NT = (((1,), (1,)), ((), ()))


HBM = pl.BlockSpec(memory_space=pltpu.HBM)
VMEM = pl.BlockSpec(memory_space=pltpu.VMEM)
SMEM = pl.BlockSpec(memory_space=pltpu.SMEM)


def fetch(src, dst, sem):
    copy = pltpu.make_async_copy(src, dst, sem)
    copy.start()
    copy.wait()


STEPS = (64, 32, 16, 8, 4, 2, 1)


def code_kernel(rows_hbm, coded, rows, sem):
    fetch(rows_hbm, rows, sem)
    owners, capacity, both = rows.shape
    feat = both // 2
    values = jnp.concatenate([rows[e].astype(jnp.float32) for e in range(owners)], axis=0)
    count = owners * capacity
    tails = []
    for i, half in enumerate((values[:, feat:], values[:, :feat])):
        largest = jnp.max(jnp.max(jnp.abs(half), axis=0, keepdims=True), axis=1, keepdims=True)
        largest = jnp.broadcast_to(largest, (1, feat))
        scale = jnp.ones((1, feat), jnp.float32)
        power = jnp.zeros((1, feat), jnp.int32)
        for step in STEPS:
            fits = largest * (2.0**step) <= 32000.0
            largest = jnp.where(fits, largest * (2.0**step), largest)
            scale = jnp.where(fits, scale * (2.0**step), scale)
            power = jnp.where(fits, power + step, power)
        whole = jnp.round(half * scale).astype(jnp.int32)
        coded[i * count : (i + 1) * count] = whole.astype(jnp.int16)
        tails.append(jnp.broadcast_to(power, (8, feat)))
    coded[2 * count :] = jnp.concatenate(tails, axis=0).astype(jnp.int16)


def code(rows):
    owners, capacity, both = rows.shape
    feat = both // 2
    return pl.pallas_call(
        code_kernel,
        out_shape=jax.ShapeDtypeStruct((2 * owners * capacity + 16, feat), jnp.int16),
        in_specs=[HBM],
        out_specs=VMEM,
        scratch_shapes=[pltpu.VMEM(rows.shape, rows.dtype), pltpu.SemaphoreType.DMA(())],
        compiler_params=pltpu.CompilerParams(vmem_limit_bytes=8 << 20),
    )(rows)


def decode(block, tail, row):
    power = tail.astype(jnp.int32)[row : row + 1]
    scale = jnp.ones(power.shape, jnp.float32)
    for step in STEPS:
        taken = power >= step
        scale = jnp.where(taken, scale * (0.5**step), scale)
        power = jnp.where(taken, power - step, power)
    return (block.astype(jnp.int32).astype(jnp.float32) * scale).astype(jnp.bfloat16)


def back_kernel(coded, down, parts, coded_v, tails_v, down_v, parts_v, sems):
    groups = parts.shape[0]
    per = coded.shape[0] // groups
    cap_rows = parts.shape[1]
    weight = pltpu.make_async_copy(down.at[0], down_v, sems.at[groups])
    tails = pltpu.make_async_copy(
        coded.at[:, pl.ds(2 * cap_rows, 16)], tails_v, sems.at[2 * groups + 1]
    )
    tails.start()
    weight.start()
    copies = [
        pltpu.make_async_copy(
            coded.at[pl.ds(per * g, per), pl.ds(0, cap_rows)], coded_v.at[g], sems.at[g]
        )
        for g in range(groups)
    ]
    for copy in copies:
        copy.start()
    tails.wait()
    weight.wait()
    sent = []
    for g in range(groups):
        copies[g].wait()
        y = jnp.concatenate([decode(coded_v[g, k], tails_v[per * g + k], 0) for k in range(per)], axis=1)
        parts_v[g] = lax.dot_general(y, down_v[...], NT, preferred_element_type=jnp.float32).astype(
            jnp.bfloat16
        )
        sent.append(pltpu.make_async_copy(parts_v.at[g], parts.at[g], sems.at[groups + 1 + g]))
        sent[g].start()
    for copy in sent:
        copy.wait()


def back_parts(coded, down, cap_rows, groups):
    blocks, lines, feat = coded.shape
    _, ff, depth = down.shape
    return pl.pallas_call(
        back_kernel,
        out_shape=pltpu.HBM((groups, cap_rows, ff), jnp.bfloat16),
        in_specs=[HBM, HBM],
        out_specs=HBM,
        scratch_shapes=[
            pltpu.VMEM((groups, blocks // groups, cap_rows, feat), jnp.int16),
            pltpu.VMEM((blocks, 16, feat), jnp.int16),
            pltpu.VMEM((ff, depth), jnp.bfloat16),
            pltpu.VMEM((groups, cap_rows, ff), jnp.bfloat16),
            pltpu.SemaphoreType.DMA((2 * groups + 2,)),
        ],
        compiler_params=pltpu.CompilerParams(vmem_limit_bytes=24 << 20),
        cost_estimate=pl.CostEstimate(
            flops=2 * groups * cap_rows * depth * ff, bytes_accessed=5 << 20, transcendentals=0
        ),
    )(coded, down)


def hidden_kernel(cap_rows, slot_of, coded, *refs):
    weights, (mixed, mixed_v, rows_v, tails_v, w_v, sems) = refs[:4], refs[4:]
    per = coded.shape[0] // 4
    ff = mixed.shape[2]
    waits = []
    for s in range(4):
        blocks = coded.at[pl.ds(slot_of[s] * per, per)]
        rows, tails = blocks.at[:, pl.ds(cap_rows, cap_rows)], blocks.at[:, pl.ds(2 * cap_rows, 16)]
        waits.append(
            [
                pltpu.make_async_copy(tails, tails_v.at[s], sems.at[9 + s]),
                pltpu.make_async_copy(rows, rows_v.at[s], sems.at[2 * s]),
                pltpu.make_async_copy(weights[s], w_v.at[s], sems.at[2 * s + 1]),
            ]
        )
        for copy in waits[s]:
            copy.start()
    total = None
    for s in range(4):
        for copy in waits[s]:
            copy.wait()
        x = jnp.concatenate([decode(rows_v[s, k], tails_v[s, k], 8) for k in range(per)], axis=1)
        part = jnp.dot(x, w_v[s], preferred_element_type=jnp.float32)
        total = part if s == 0 else total + part
    gate_pre, up_pre = total[:, :ff], total[:, ff:]
    sig = 1.0 / (1.0 + jnp.exp(-gate_pre))
    act = gate_pre * sig
    mixed_v[0] = up_pre * sig * (1.0 + gate_pre * (1.0 - sig))
    mixed_v[1] = act
    mixed_v[2] = act * up_pre
    sent = pltpu.make_async_copy(mixed_v, mixed, sems.at[8])
    sent.start()
    sent.wait()


def hidden_part(coded, weights, slot_of, cap_rows):
    blocks, lines, feat = coded.shape
    depth, wide = weights[0].shape
    return pl.pallas_call(
        functools.partial(hidden_kernel, cap_rows),
        out_shape=pltpu.HBM((3, cap_rows, wide // 2), jnp.float32),
        in_specs=[SMEM] + [HBM] * 5,
        out_specs=HBM,
        scratch_shapes=[
            pltpu.VMEM((3, cap_rows, wide // 2), jnp.float32),
            pltpu.VMEM((4, blocks // 4, cap_rows, feat), jnp.int16),
            pltpu.VMEM((4, blocks // 4, 16, feat), jnp.int16),
            pltpu.VMEM((4, depth, wide), jnp.bfloat16),
            pltpu.SemaphoreType.DMA((13,)),
        ],
        compiler_params=pltpu.CompilerParams(vmem_limit_bytes=32 << 20),
        cost_estimate=pl.CostEstimate(
            flops=8 * cap_rows * depth * wide,
            bytes_accessed=12 << 20,
            transcendentals=cap_rows * wide // 2,
        ),
    )(slot_of, coded, *weights)


def term_kernel(pitch, slots, slot_of, z_of, mixed_hbm, backs_hbm, *refs):
    weights, (out, mixed, backs, w_v, out_v, blank, sems) = refs[:4], refs[4:]
    cap_rows = mixed.shape[1]
    feat = out.shape[1]
    per = w_v.shape[1] // feat
    first = [
        pltpu.make_async_copy(backs_hbm, backs, sems.at[4]),
        pltpu.make_async_copy(mixed_hbm, mixed, sems.at[5]),
    ]
    for copy in first:
        copy.start()
    waits = [pltpu.make_async_copy(weights[s], w_v.at[s], sems.at[s]) for s in range(4)]
    for copy in waits:
        copy.start()
    for copy in first:
        copy.wait()
    for s in range(4):
        b = backs[s].astype(jnp.float32)
        back = b if s == 0 else back + b
    prod = mixed[2] * back
    sides = jnp.concatenate(
        [(back * mixed[0]).astype(jnp.bfloat16), (back * mixed[1]).astype(jnp.bfloat16)], axis=1
    )

    prod = sum(prod[:, 128 * i : 128 * (i + 1)] for i in range(prod.shape[1] // 128))
    ones = jnp.ones((16, prod.shape[1]), jnp.bfloat16)
    total = None
    rest = prod
    for _ in range(3):
        limb = rest.astype(jnp.bfloat16)
        rest = rest - limb.astype(jnp.float32)
        part = lax.dot_general(ones, limb, NT, preferred_element_type=jnp.float32)
        total = part if total is None else total + part
    top = total.astype(jnp.bfloat16).astype(jnp.float32)
    low = total - top
    over = cap_rows - feat
    row = lax.broadcasted_iota(jnp.int32, (16, feat), 0)
    lane = lax.broadcasted_iota(jnp.int32, (16, feat), 1)
    q = z_of[0]
    mine = (lane >= q * over) & (lane < (q + 1) * over)
    wide = lambda v: jnp.concatenate([v[:, feat:]] * (feat // over), axis=1)
    extra = jnp.where(row == q, top[:, :feat], 0.0)
    extra = jnp.where(row == q + slots, low[:, :feat], extra)
    extra = jnp.where((row == 2 * slots) & mine, wide(top), extra)
    extra = jnp.where((row == 2 * slots + 1) & mine, wide(low), extra)
    extra = extra.astype(jnp.bfloat16)
    tail = pitch - cap_rows - 16
    span = per * pitch - tail
    blank[...] = jnp.zeros(blank.shape, blank.dtype)
    sent = []
    for j in range(3):
        sent.append(
            pltpu.make_async_copy(
                blank, out.at[pl.ds(j * per * pitch + span, tail)], sems.at[11 + j]
            )
        )
        sent[j].start()
    for s in range(4):
        waits[s].wait()
        term = lax.dot_general(sides, w_v[s], NT, preferred_element_type=jnp.float32)
        for k in range(per):
            at = k * pitch
            out_v[s, at : at + cap_rows] = term[:, k * feat : (k + 1) * feat].astype(jnp.bfloat16)
            out_v[s, at + cap_rows : at + cap_rows + 16] = extra
            if k + 1 < per:
                out_v[s, at + cap_rows + 16 : at + pitch] = jnp.zeros((tail, feat), jnp.bfloat16)
        at = pl.multiple_of(slot_of[s] * (per * pitch), 16)
        sent.append(pltpu.make_async_copy(out_v.at[s], out.at[pl.ds(at, span)], sems.at[7 + s]))
        sent[3 + s].start()
    for copy in sent:
        copy.wait()


def term_part(mixed, backs, weights, slot_of, z_index, feat, pitch, out_rows, slots):
    _, cap_rows, ff = mixed.shape
    depth, wide = weights[0].shape
    z_of = jnp.reshape(z_index % slots, (1,)).astype(jnp.int32)
    per = depth // feat
    return pl.pallas_call(
        functools.partial(term_kernel, pitch, slots),
        out_shape=pltpu.HBM((out_rows, feat), jnp.bfloat16),
        in_specs=[SMEM, SMEM] + [HBM] * 6,
        out_specs=HBM,
        scratch_shapes=[
            pltpu.VMEM((3, cap_rows, ff), jnp.float32),
            pltpu.VMEM((4, cap_rows, ff), jnp.bfloat16),
            pltpu.VMEM((4, depth, wide), jnp.bfloat16),
            pltpu.VMEM((4, per * pitch - 16, feat), jnp.bfloat16),
            pltpu.VMEM((16, feat), jnp.bfloat16),
            pltpu.SemaphoreType.DMA((14,)),
        ],
        compiler_params=pltpu.CompilerParams(vmem_limit_bytes=40 << 20),
        cost_estimate=pl.CostEstimate(
            flops=8 * cap_rows * depth * wide, bytes_accessed=14 << 20, transcendentals=0
        ),
    )(slot_of, z_of, mixed, backs, *weights)


def tag_kernel(out_grad, routes, tagged):
    tok_rows, feat = out_grad.shape
    tagged[:tok_rows] = out_grad[...]
    lines = routes[...].astype(jnp.float32)
    lines = jnp.concatenate([lines, jnp.zeros((2, feat - tok_rows), jnp.float32)], axis=1)
    row = lax.broadcasted_iota(jnp.int32, (16, feat), 0)
    tags = jnp.where(row == 0, lines[0:1], jnp.where(row == 1, lines[1:2], 0.0))
    tagged[tok_rows:] = tags.astype(jnp.bfloat16)


def tag(out_grad, routes):
    tok_rows, feat = out_grad.shape
    return pl.pallas_call(
        tag_kernel,
        out_shape=jax.ShapeDtypeStruct((tok_rows + 16, feat), jnp.bfloat16),
        in_specs=[VMEM, VMEM],
        out_specs=VMEM,
        compiler_params=pltpu.CompilerParams(vmem_limit_bytes=8 << 20),
    )(pltpu.with_memory_space_constraint(out_grad, pltpu.HBM), routes)


def place_kernel(capacity, routes, tokens, moved_hbm, placed, slot, moved, sem):
    fetch(moved_hbm, moved, sem)
    tok_rows, feat = tokens.shape
    experts = placed.shape[0]
    ids = lax.broadcasted_iota(jnp.int32, (16, tok_rows), 0)
    place_of = lax.broadcasted_iota(jnp.int32, (48, tok_rows), 0)
    before = lax.broadcasted_iota(jnp.int32, (tok_rows, tok_rows), 0) < lax.broadcasted_iota(
        jnp.int32, (tok_rows, tok_rows), 1
    )
    as_ones = lambda mask: jnp.where(mask, 1.0, 0.0).astype(jnp.bfloat16)

    def slots_of(first, second):
        hot = (first == ids) | (second == ids)
        ranks = jnp.dot(as_ones(hot), as_ones(before), preferred_element_type=jnp.float32)
        return [
            jnp.sum(jnp.where(r == ids, ranks, 0.0), axis=0, keepdims=True).astype(jnp.int32)
            for r in (first, second)
        ]

    far = moved[tok_rows:].astype(jnp.float32).astype(jnp.int32)
    kinds = []
    for first, second, rows in (
        (routes[0:1, :], routes[1:2, :], tokens[...]),
        (far[0:1, :tok_rows], far[1:2, :tok_rows], moved[:tok_rows]),
    ):
        kinds.append((first, second, slots_of(first, second), rows))
    slot[...] = jnp.concatenate(kinds[0][2], axis=0)
    for e in range(experts):
        found = []
        for first, second, slots, rows in kinds:
            wanted = jnp.where(first == e, slots[0], jnp.where(second == e, slots[1], -1))
            found.append(
                jnp.dot(as_ones(wanted == place_of), rows, preferred_element_type=jnp.float32)
            )
        placed[e] = jnp.concatenate(found, axis=1)[:capacity].astype(jnp.bfloat16)


def place(routes, tokens, moved, experts, capacity):
    tok_rows, feat = tokens.shape
    vmem = pl.BlockSpec(memory_space=pltpu.VMEM)
    return pl.pallas_call(
        functools.partial(place_kernel, capacity),
        out_shape=(
            jax.ShapeDtypeStruct((experts, capacity, 2 * feat), jnp.bfloat16),
            jax.ShapeDtypeStruct((2, tok_rows), jnp.int32),
        ),
        in_specs=[vmem, vmem, HBM],
        out_specs=(vmem, vmem),
        scratch_shapes=[pltpu.VMEM(moved.shape, moved.dtype), pltpu.SemaphoreType.DMA(())],
        compiler_params=pltpu.CompilerParams(vmem_limit_bytes=8 << 20),
    )(routes, tokens, moved)


def pack_kernel(owners, capacity, slots, z_of, summed, payload, wide):
    feat = summed.shape[1]
    cap_rows = owners * capacity
    over = cap_rows - feat
    count = wide.shape[0]
    wide[pl.ds(0, summed.shape[0]), :] = summed[...].astype(jnp.float32)
    lined = pltpu.roll(wide[...], lax.rem(count - z_of[0], count), 0)
    extra = lined[cap_rows : cap_rows + 16]
    row = lax.broadcasted_iota(jnp.int32, (16, feat), 0)
    lane = lax.broadcasted_iota(jnp.int32, (16, feat), 1)
    head = jnp.sum(jnp.where(row < 2 * slots, extra, 0.0), axis=0, keepdims=True)
    tail = jnp.sum(
        jnp.where((row >= 2 * slots) & (lane < slots * over), extra, 0.0), axis=0, keepdims=True
    )
    tail = sum(tail[:, over * q : over * (q + 1)] for q in range(slots))
    gates = jnp.concatenate([head, tail], axis=1)
    top = gates.astype(jnp.bfloat16).astype(jnp.float32)
    low = gates - top
    blank = jnp.zeros((1, feat - 2 * capacity), jnp.float32)
    rest = jnp.zeros((payload.shape[1] - capacity - 1, feat), jnp.float32)
    for d in range(owners):
        cut = slice(capacity * d, capacity * (d + 1))
        line = jnp.concatenate([top[:, cut], low[:, cut], blank], axis=1)
        rows = lined[capacity * d : capacity * (d + 1)]
        payload[d] = jnp.concatenate([rows, line, rest], axis=0).astype(jnp.bfloat16)


def pack(summed, z_index, owners, capacity, slots, lines):
    rows, feat = summed.shape
    vmem = pl.BlockSpec(memory_space=pltpu.VMEM)
    return pl.pallas_call(
        functools.partial(pack_kernel, owners, capacity, slots),
        out_shape=jax.ShapeDtypeStruct((owners, lines, feat), jnp.bfloat16),
        in_specs=[pl.BlockSpec(memory_space=pltpu.SMEM), vmem],
        out_specs=vmem,
        scratch_shapes=[pltpu.VMEM((rows + 1, feat), jnp.float32)],
    )(jnp.reshape(z_index, (1,)).astype(jnp.int32), summed)


def combine_kernel(capacity, routes, slot, probs, came_hbm, input_grad, gate_grad, came, sem):
    fetch(came_hbm, came, sem)
    tok_rows = routes.shape[1]
    experts, lines, feat = came.shape
    flat = came[...].reshape(experts * lines, feat)
    place_of = lax.broadcasted_iota(jnp.int32, (experts * lines, tok_rows), 0)
    weight = jnp.zeros(place_of.shape, jnp.float32)
    for k in range(2):
        at = routes[k : k + 1, :] * lines + slot[k : k + 1, :]
        weight = jnp.where(place_of == at, probs[k : k + 1, :], weight)
    total = None
    for _ in range(3):
        limb = weight.astype(jnp.bfloat16)
        weight = weight - limb.astype(jnp.float32)
        part = lax.dot_general(
            limb, flat, (((0,), (0,)), ((), ())), preferred_element_type=jnp.float32
        )
        total = part if total is None else total + part
    input_grad[...] = total.astype(jnp.bfloat16)

    gates = jnp.concatenate(
        [came[e, 32:48].astype(jnp.float32)[capacity - 32 : capacity - 31] for e in range(experts)], axis=0
    ).astype(jnp.bfloat16)
    lane_of = lax.broadcasted_iota(jnp.int32, (feat, tok_rows), 0)
    ids = lax.broadcasted_iota(jnp.int32, (experts, tok_rows), 0)
    lines_of = []
    for k in range(2):
        s = slot[k : k + 1, :]
        pick = jnp.where((lane_of == s) | (lane_of == s + capacity), 1.0, 0.0).astype(jnp.bfloat16)
        values = jnp.dot(gates, pick, preferred_element_type=jnp.float32)
        lines_of.append(
            jnp.sum(jnp.where(routes[k : k + 1, :] == ids, values, 0.0), axis=0, keepdims=True)
        )
    gate_grad[...] = jnp.concatenate(lines_of, axis=0)


def combine(routes, slot, probs, came, capacity):
    tok_rows = routes.shape[1]
    feat = came.shape[2]
    vmem = pl.BlockSpec(memory_space=pltpu.VMEM)
    return pl.pallas_call(
        functools.partial(combine_kernel, capacity),
        out_shape=(
            jax.ShapeDtypeStruct((tok_rows, feat), jnp.bfloat16),
            jax.ShapeDtypeStruct((2, tok_rows), jnp.float32),
        ),
        in_specs=[vmem] * 3 + [HBM],
        out_specs=(vmem, vmem),
        scratch_shapes=[pltpu.VMEM(came.shape, came.dtype), pltpu.SemaphoreType.DMA(())],
        compiler_params=pltpu.CompilerParams(vmem_limit_bytes=8 << 20),
    )(routes, slot, probs, came)


def trade(value, axis, bits):
    return lax.ppermute(value, axis, [(i, i ^ bits) for i in range(lax.axis_size(axis))])


def shards(tokens, out_grad, routes, gate_probs, gate_weight, up_weight, down_weight):
    tok_rows, feat = tokens.shape
    owners = lax.axis_size("expert")
    blocks = lax.axis_size("etensor")
    experts = owners * gate_weight.shape[0]
    capacity = min(tok_rows, 9 * tok_rows // (4 * experts))
    x_index = lax.axis_index("dp")
    z_index = lax.axis_index("etensor")
    cap_rows = owners * capacity
    slots = 7

    columns = lax.axis_size("dp")
    gate_up = jnp.concatenate([gate_weight[0], up_weight[0]], axis=1)

    per = blocks // columns
    swap = [
        ((columns * a + w) * columns + x, (columns * x + w) * columns + a)
        for a in range(columns)
        for w in range(per)
        for x in range(columns)
    ]
    moved = lax.ppermute(tag(out_grad, routes.T), ("etensor", "dp"), swap)

    def send():
        placed, slot = place(routes.T, tokens, moved, experts, capacity)
        part = lax.all_to_all(placed, "expert", split_axis=0, concat_axis=0, tiled=True)
        return code(part), slot

    coded, slot = lax.cond(
        x_index >= 0,
        send,
        lambda: (
            jnp.zeros((2 * cap_rows + 16, feat), jnp.int16),
            jnp.zeros((2, tok_rows), jnp.int32),
        ),
    )
    coded = lax.all_gather(coded, "etensor", axis=0, tiled=False)
    coded = pltpu.with_memory_space_constraint(coded, pltpu.HBM)
    backs = lax.all_to_all(
        back_parts(coded, down_weight, cap_rows, columns), "dp", split_axis=0, concat_axis=0, tiled=True
    )

    weights = (gate_up,) + tuple(trade(gate_up, "dp", bits) for bits in (2, 1, 3))
    slot_of = jnp.stack([x_index ^ bits for bits in (0, 2, 1, 3)]).astype(jnp.int32)
    mixed = pltpu.with_memory_space_constraint(
        hidden_part(coded, weights, slot_of, cap_rows), pltpu.HBM
    )
    pitch = cap_rows + 32
    terms = term_part(
        mixed, backs, weights, slot_of, z_index, feat, pitch, blocks * (pitch - 1), slots
    )
    summed = lax.psum_scatter(terms, "etensor", scatter_dimension=0, tiled=True)
    payload = pack(summed, z_index, owners, capacity, slots, 48)
    came = lax.all_to_all(payload, "expert", split_axis=0, concat_axis=0, tiled=True)
    input_grad, gate_grad = combine(routes.T, slot, gate_probs.T, came, capacity)
    return input_grad, gate_grad.T


def solution(mesh):
    return jax.shard_map(
        shards,
        mesh=mesh,
        in_specs=(
            P(("expert", "dp"), "etensor"),
            P(("expert", "dp"), "etensor"),
            P(("expert", "dp"), None),
            P(("expert", "dp"), None),
            P("expert", "dp", "etensor"),
            P("expert", "dp", "etensor"),
            P("expert", "etensor", "dp"),
        ),
        out_specs=(P(("expert", "dp"), "etensor"), P(("expert", "dp"), None)),
        check_vma=False,
    )
```
